512 devices in a mesh: row: 16 (over y, core), col: 32 (over z, x).
Axes of the slice: x: 4, y: 8, z: 8, core: 2. Of those that a mesh axis runs over, the one named last changes fastest.
Arguments:
- feats: bfloat16 [512, 131072], P('col', 'row'), may hold values from -6 to 6
- weight: bfloat16 [512, 512], replicated, may hold values from -0.25 to 0.25
- tile_vals: bfloat16 [16384, 128, 128], P(('row', 'col')), may hold values from -0.125 to 0.125
- tile_src: int32 [512, 32], P(('row', 'col')), may hold values from 0 to 1, as said below
- tile_slot: int32 [512, 32], P(('row', 'col')), may hold values from 0 to 31, as said below
- slot_block: int32 [512, 32], replicated, may hold values from 0 to 63
- cotangent: bfloat16 [512, 131072], P('col', 'row'), may hold values from -6 to 6
Outputs:
- mixed: bfloat16 [512, 131072], P('col', 'row')
- feat_grad: bfloat16 [512, 131072], P('col', 'row')
- weight_grad: float32 [512, 512], replicated
The draws below stay inside these ranges and needn't reach their ends.
Inputs may be any that keep to these rules, and one draw needn't show every extreme that they name: The tiles of one device name distinct (tile_src, tile_slot) pairs; slots of the device's own row group are all named. tile_slot // 2 is the destination row group of a tile; some tile of every device names slot 31 and some names slot 0. `slot_block`: two slots may target the same block.
All inputs are finite; a program needn't handle non-finite values.
Results may differ from the reference program's by a relative error of at most 0.007.
Values may be sent and summed in bfloat16 or wider, within the bound.
A program may use at most 128 MiB of HBM per device.

```python
import math
import jax
import jax.numpy as jnp
from jax import lax

F = 512
BLK = 128
NB_DEV = 2
CAP = 2
SLOTS = 32
TILES = 32
NODES = 131072
N_ROW = 16
N_COL = 32
DEVICES = 512


def pick_pairs(key):
    slots = N_ROW * CAP
    pairs = NB_DEV * slots
    devices = N_ROW * N_COL
    noise = jax.random.randint(key, (devices, pairs), 0, 1 << 20)
    pair_index = jnp.arange(pairs, dtype=jnp.int32)
    own_group = (jnp.arange(devices, dtype=jnp.int32) // N_COL)[:, None]
    nearby = ((pair_index % slots // CAP)[None, :] == own_group).astype(jnp.int32)
    forced = ((pair_index == pairs - 1) | (pair_index == 0)).astype(jnp.int32)[None, :]
    score = (noise + nearby * (1 << 20) + forced * (1 << 21)) * pairs + pair_index[None, :]
    _, chosen = lax.top_k(score, TILES)
    return chosen.astype(jnp.int32)


def draw_tile_src(key, part):
    chosen = pick_pairs(key)
    return (chosen // (N_ROW * CAP)).astype(jnp.int32)


def draw_tile_slot(key, part):
    chosen = pick_pairs(key)
    return (chosen % (N_ROW * CAP)).astype(jnp.int32)


def plant(entries, stream_key, least, largest):
    extent = entries.shape
    index_at = [jax.random.randint(jax.random.fold_in(stream_key, axis), (), 0, extent[axis]) for axis in range(len(extent))]
    entries = entries.at[tuple(index_at)].set(least)
    longest = extent.index(max(extent))
    index_at[longest] = (index_at[longest] + 1) % extent[longest]
    return entries.at[tuple(index_at)].set(largest)


def shard_levels(key, dims, pieces, least, high):
    level, own = 1.0, jax.random.fold_in(key, 6)
    for dim, shards_of in pieces:
        heights = jnp.exp(jax.random.uniform(jax.random.fold_in(own, dim), (shards_of,), jnp.float32, least / len(pieces), high / len(pieces)))
        level = level * jnp.repeat(heights, dims[dim] // shards_of).reshape([-1 if axis == dim else 1 for axis in range(len(dims))])
    return level


def centred(stream_key, dims, width, most, split=(), held_as=jnp.bfloat16):
    gain = shard_levels(stream_key, dims, split, -0.22, 0.18) if split else 1.0
    result = jax.random.normal(stream_key, dims, jnp.float32) * width * gain
    return jnp.minimum(jnp.maximum(result, -most), most).astype(held_as)


def setup_inputs(seed: int = 0) -> dict:
    key_of = jax.random.split(jax.random.key(seed), 8)
    feats = centred(key_of[0], (F, NODES), 1.0, 6.0, ((0, 32), (1, 16)))
    weight = centred(key_of[1], (F, F), F ** -0.5, 0.25)
    tile_vals = centred(key_of[2], (DEVICES * TILES, BLK, BLK), (TILES * BLK // NB_DEV) ** -0.5, 0.125, ((0, 512),))
    tile_src = draw_tile_src(jax.random.fold_in(key_of[7], 71), 0)
    tile_slot = draw_tile_slot(jax.random.fold_in(key_of[7], 71), 0)
    slot_block = plant(jax.random.randint(key_of[5], (DEVICES, SLOTS), 0, N_COL * NB_DEV), jax.random.fold_in(key_of[5], 1), 0, (N_COL * NB_DEV) - 1).astype(jnp.int32)
    cotangent = centred(key_of[6], (F, NODES), 1.0, 6.0, ((0, 32), (1, 16)))
    return {"feats": feats, "weight": weight, "tile_vals": tile_vals, "tile_src": tile_src, "tile_slot": tile_slot, "slot_block": slot_block, "cotangent": cotangent}


def reference(feats, weight, tile_vals, tile_src, tile_slot, slot_block, cotangent):
    devices = N_ROW * N_COL
    group_blocks = N_COL * NB_DEV
    node_major = feats.T
    projected = jnp.dot(node_major, weight, preferred_element_type=jnp.float32).astype(jnp.bfloat16)
    y_devices = projected.reshape(devices, NB_DEV, BLK, F)
    tile_devices = tile_vals.reshape(devices, TILES, BLK, BLK)
    slot_ids = jnp.arange(SLOTS, dtype=jnp.int32)
    block_ids = jnp.arange(NB_DEV, dtype=jnp.int32)
    slot_group = slot_ids // CAP * group_blocks

    def forward_step(carry, inputs):
        y_here, tiles_here, sources, targets, blocks = inputs
        picked = y_here[sources].astype(jnp.float32)
        product = jnp.einsum('tds,tsf->tdf', tiles_here.astype(jnp.float32), picked)
        onehot = (targets[:, None] == slot_ids[None, :]).astype(jnp.float32)
        partial_value = jnp.einsum('tdf,ts->sdf', product, onehot, precision=lax.Precision.HIGHEST).astype(jnp.bfloat16)
        carry = carry.at[slot_group + blocks].add(partial_value.astype(jnp.float32))
        return (carry, None)
    pre_blocks, _ = lax.scan(forward_step, jnp.zeros((NODES // BLK, BLK, F), jnp.float32), (y_devices, tile_devices, tile_src, tile_slot, slot_block))
    pre = pre_blocks.reshape(NODES, F)
    sigma = jax.nn.sigmoid(pre)
    mixed = (pre * sigma).astype(jnp.bfloat16).T
    grad_pre = (cotangent.T.astype(jnp.float32) * sigma * (1.0 + pre * (1.0 - sigma))).astype(jnp.bfloat16)
    grad_blocks = grad_pre.reshape(NODES // BLK, BLK, F)

    def backward_one(inputs):
        tiles_here, sources, targets, blocks = inputs
        gathered = grad_blocks[slot_group + blocks]
        taken = gathered[targets].astype(jnp.float32)
        product = jnp.einsum('tds,tdf->tsf', tiles_here.astype(jnp.float32), taken)
        onehot = (sources[:, None] == block_ids[None, :]).astype(jnp.float32)
        summed = jnp.einsum('tsf,tb->bsf', product, onehot, precision=lax.Precision.HIGHEST)
        return summed.reshape(NB_DEV * BLK, F).astype(jnp.bfloat16)
    grad_y = lax.map(backward_one, (tile_devices, tile_src, tile_slot, slot_block)).reshape(NODES, F)
    weight_grad = jnp.dot(feats, grad_y, preferred_element_type=jnp.float32) / math.sqrt(NODES)
    feat_grad = jnp.dot(weight, grad_y.T, preferred_element_type=jnp.float32).astype(jnp.bfloat16)
    return (mixed, feat_grad, weight_grad)
```

```python
import functools
import math
import types

import jax
import jax.numpy as jnp
from jax import lax
from jax.experimental import pallas as pl
from jax.experimental.pallas import tpu as pltpu
from jax.sharding import PartitionSpec as P

BF = jnp.bfloat16
F32 = jnp.float32
MESH = pl.DeviceIdType.MESH
NK = 2
CAP = 2
BLK = 128
LIMIT = 56 * 1024 * 1024


class Dims:
    def __init__(self, n_row, n_col):
        self.nrow, self.ncol = n_row, n_col
        self.nx = 4 if n_col > 4 else 2
        self.ny, self.nz = n_row // NK, n_col // self.nx
        self.width = 16 * n_col
        self.blocks = 2 * n_col
        self.slots = CAP * n_row
        self.na = NK * n_col
        self.nb = n_row * self.nx
        self.ncol_b = self.nb // NK
        self.slot_devices = n_row * n_col
        assert self.na == self.nb

    def here(self):
        r, c = lax.axis_index("row"), lax.axis_index("col")
        return r, c, r // NK, lax.rem(r, NK), c // self.nx, lax.rem(c, self.nx)


def remote(src, dst, send_sem, recv_sem, row, col):
    return pltpu.make_async_remote_copy(
        src_ref=src,
        dst_ref=dst,
        send_sem=send_sem,
        recv_sem=recv_sem,
        device_id=(row, col),
        device_id_type=MESH,
    )


def drain(ref, sem):
    pltpu.make_async_copy(ref, ref, sem).wait()


def each(start, stop, step):
    def run(i, carry):
        step(i)
        return carry

    lax.fori_loop(start, stop, run, 0)


def greet(barrier, row, col):
    pl.semaphore_signal(barrier, inc=1, device_id=(row, col), device_id_type=MESH)


def tile_of(inv, tiles, group, cap, source):
    at = inv[(group * CAP + cap) * 2 + source]
    value = tiles[jnp.maximum(at, 0)]
    return jnp.where(at >= 0, value, jnp.zeros_like(value))


def ways(n, way, piece):
    return n // 2 if way == piece else (n - 1) // 2


def offset_of(pos, n):
    if pos == 0:
        return n // 2
    return n // 2 - (pos + 1) // 2 if pos % 2 else -(n // 2 - pos // 2)


def pos_of(offset, n):
    if isinstance(offset, int):
        return [p for p in range(n) if (offset_of(p, n) - offset) % n == 0][0]
    return jnp.where(offset > n // 2, 2 * offset - n, jnp.maximum(n - 1 - 2 * offset, 0))


def far_count(n):
    return max(1, n - 3)


def near_start(n):
    return max(1, n - 5)


class Ring:
    def __init__(self, n, me, rows, device, send, recv, recv_gather):
        self.n, self.me, self.half, self.device = n, me, rows // 2, device
        self.send, self.recv, self.recv_gather = send, recv, recv_gather
        self.hops = max(1, n // 2)

    def at(self, way, piece, step):
        return (way * 2 + piece) * self.hops + step

    def rows(self, piece):
        return pl.ds(piece * self.half, self.half)

    def near(self, offset):
        return lax.rem(self.me + offset + self.n, self.n)

    def copies(self):
        return sum(ways(self.n, w, p) for w in range(2) for p in range(2))

    def start(self, src, dst, way, piece, step, recv):
        row, col = self.device(self.near(1 - 2 * way))
        at = self.at(way, piece, step)
        remote(src, dst, self.send.at[0], recv.at[at], row, col).start()

    def reduce_step(self, step, dense, got, stage, last):
        for piece in range(2):
            for way in range(2):
                hops = ways(self.n, way, piece)
                if step >= hops:
                    continue
                to = pos_of((1 - 2 * way) * (hops - step), self.n)
                if (to >= far_count(self.n)) != last:
                    continue
                if step == 0:
                    src = dense.at[to, self.rows(piece)]
                else:
                    old = self.at(way, piece, step - 1)
                    drain(got.at[old], self.recv.at[old])
                    new = self.at(way, piece, step)
                    total = got[old].astype(F32) + dense[to, self.rows(piece)].astype(F32)
                    stage[new] = total.astype(BF)
                    src = stage.at[new]
                self.start(src, got.at[self.at(way, piece, step)], way, piece, step, self.recv)

    def reduce_end(self, piece, got):
        ends = []
        for way in range(2):
            hops = ways(self.n, way, piece)
            if hops:
                at = self.at(way, piece, hops - 1)
                drain(got.at[at], self.recv.at[at])
                ends.append(at)
        return ends

    def gather_step(self, step, piece, held, widen):
        for way in range(2):
            hops = ways(self.n, way, piece)
            if step > hops or hops == 0:
                continue
            src = self.near(-(1 - 2 * way) * step)
            pos = pos_of(-(1 - 2 * way) * step, self.n)
            part = held.at[src, self.rows(piece)]
            if step:
                drain(part, self.recv_gather.at[self.at(way, piece, step - 1)])
            if step < hops:
                self.start(part, part, way, piece, step, self.recv_gather)
            if step:
                widen(src, pos, piece)


def whole_kernel(d, scale, names, *refs):
    m = types.SimpleNamespace(**dict(zip(names, refs)))
    r, c, y, k, z, x = d.here()
    me_a, me_b = k * d.ncol + c, r * d.nx + x
    half = d.width // 2
    send, recv = m.send, m.recv
    barrier = pltpu.get_barrier_semaphore()

    def turn(i, n):
        j = (i + 1) // 2
        return jnp.where(lax.rem(i, 2) == 1, j, lax.rem(n - j, n))

    def peer_col(i):
        to_z = lax.rem(z + turn(i // d.nx, d.nz), d.nz)
        return to_z * d.nx + lax.rem(x + i, d.nx)

    def peer_a(i):
        return lax.rem(k + i // d.ncol, NK), peer_col(lax.rem(i, d.ncol))

    def peer_b(i):
        j = lax.rem(i, d.ncol_b)
        to_y = lax.rem(y + turn(j // d.nx, d.ny), d.ny)
        return to_y * NK + lax.rem(k + i // d.ncol_b, NK), lax.rem(x + j, d.nx)

    def hello(i):
        to_k, to_col = peer_a(i)
        greet(barrier, y * NK + to_k, to_col)
        to_row, to_x = peer_b(i)
        greet(barrier, to_row, z * d.nx + to_x)

    each(1, d.na, hello)

    def place(group):
        offset = lax.rem(group // NK - y + d.ny, d.ny)
        at = pl.multiple_of((lax.rem(group, NK) * d.ny + pos_of(offset, d.ny)) * BLK, BLK)
        for cap in range(CAP):
            for s in range(2):
                lanes = slice((cap * 2 + s) * BLK, (cap * 2 + s + 1) * BLK)
                m.matrix[pl.ds(at, BLK), lanes] = tile_of(m.inv, m.tiles, group, cap, s)

    pl.semaphore_wait(barrier, d.na - 1 + d.nb - 1)

    def nodes_of(col):
        return m.feats.at[:, pl.ds(pl.multiple_of(col * 256, 256), 256)]

    own_rows = m.slab.at[pl.ds(pl.multiple_of(c * 16, 16), 16)]
    pltpu.make_async_copy(nodes_of(c), own_rows, recv.at[0]).start()

    def send_feats(i):
        to = peer_col(i)
        remote(nodes_of(to), own_rows, send.at[0], recv.at[0], r, to).start()

    each(1, d.ncol, send_feats)
    each(0, d.nrow, place)
    m.weight_t[...] = m.weight[...].T
    drain(m.slab, recv.at[0])
    value = jnp.dot(m.weight_t[...], m.slab[...], preferred_element_type=F32)
    value = value.reshape(d.ncol, 2, 8, 256)
    value = jnp.concatenate([value[:, 0], value[:, 1]], axis=0)
    m.proj[...] = value.reshape(d.width, 256).astype(BF)

    far_a, far_b = far_count(d.ny), far_count(d.nz)
    lanes_of = [
        pl.ds(pl.multiple_of(pos_of(lax.rem(j - z + d.nz, d.nz), d.nz) * BLK, BLK), BLK)
        for j in range(d.nz)
    ]
    x_of = [lax.rem(x + j, d.nx) for j in range(d.nx)]

    def send_b(group, late):
        lanes = pl.ds(far_b * BLK, (d.nz - far_b) * BLK) if late else pl.ds(0, far_b * BLK)
        sem = 3 if late else 2

        def send_to(to_x):
            src = m.out_b.at[group * d.nx + to_x, :, lanes]
            dst = m.got_b.at[pl.ds(pl.multiple_of(me_b * 16, 16), 16), lanes]
            remote(src, dst, send.at[sem], recv.at[sem], group, z * d.nx + to_x).start()

        @pl.when(group != r)
        def _():
            send_to(x)

        for j in range(1, d.nx):
            send_to(x_of[j])

    def group_step(gk, pos):
        gy = lax.rem(y + offset_of(pos, d.ny) + d.ny, d.ny)
        group = gy * NK + gk
        at = pl.multiple_of((gk * d.ny + pos) * BLK, BLK)
        both = jnp.concatenate(
            [m.matrix[pl.ds(at, BLK), : 2 * BLK], m.matrix[pl.ds(at, BLK), 2 * BLK :]], axis=0
        )
        part = lax.dot_general(
            m.proj[...], both, (((1,), (1,)), ((), ())), preferred_element_type=F32
        )
        first = part[:, :BLK].reshape(2 * d.ncol, 8, BLK)
        second = part[:, BLK:].reshape(2 * d.ncol, 8, BLK)
        packed = jnp.concatenate([first, second], axis=1).astype(BF)
        m.out_a[pl.ds(gk * d.ncol, d.ncol), pos] = packed[: d.ncol]
        for to_x in range(d.nx):
            for to_z in range(d.nz):
                m.out_b[group * d.nx + to_x, :, lanes_of[to_z]] = packed[
                    d.ncol + to_z * d.nx + to_x
                ]
        send_b(group, False)

    def send_a(i, late):
        to_k, to = peer_a(i)
        part = pl.ds(far_a, d.ny - far_a) if late else pl.ds(0, far_a)
        sem = 12 if late else 1
        remote(
            m.out_a.at[to_k * d.ncol + to, part],
            m.got_a.at[part, pl.ds(pl.multiple_of(me_a * 16, 16), 16)],
            send.at[sem], recv.at[sem], y * NK + to_k, to,
        ).start()

    for late in range(2):
        for first_k in range(2):
            gk = k if first_k == 0 else 1 - k
            for pos in range(far_a, d.ny) if late else range(far_a):
                group_step(gk, pos)
            if not late:
                each(max(1, first_k * d.ncol), (first_k + 1) * d.ncol, lambda i: send_a(i, False))
    each(0, d.nrow, lambda i: send_b(lax.rem(r + i, d.nrow), True))
    each(1, d.na, lambda i: send_a(i, True))
    for late in range(2):
        part = pl.ds(far_a, d.ny - far_a) if late else pl.ds(0, far_a)
        pltpu.make_async_copy(
            m.out_a.at[me_a, part],
            m.got_a.at[part, pl.ds(pl.multiple_of(me_a * 16, 16), 16)],
            recv.at[12 if late else 1],
        ).start()
        lanes = pl.ds(far_b * BLK, (d.nz - far_b) * BLK) if late else pl.ds(0, far_b * BLK)
        pltpu.make_async_copy(
            m.out_b.at[me_b, :, lanes],
            m.got_b.at[pl.ds(pl.multiple_of(me_b * 16, 16), 16), lanes],
            recv.at[3 if late else 2],
        ).start()

    lane = lax.broadcasted_iota(jnp.int32, (d.slot_devices, d.na * 16), 1)
    device = lax.broadcasted_iota(jnp.int32, (d.slot_devices, d.na * 16), 0)
    src = lane // 16
    table = m.slot_table[...].astype(F32).astype(BF)
    row_lane = lax.broadcasted_iota(jnp.int32, (1, d.na * 16), 1)
    slot_id = lax.broadcasted_iota(jnp.int32, (d.slots, d.na * 16), 0)
    slot_lane = lax.broadcasted_iota(jnp.int32, (d.slots, d.na * 16), 1)
    lane_cap = lax.rem(slot_lane, 16) // 8
    feature = lax.rem(row_lane, 8).astype(F32)

    def targets(owner):
        onehot = jnp.where(device == owner, 1.0, 0.0).astype(BF)
        m.spread_slots[...] = lax.dot_general(
            table, onehot, (((0,), (0,)), ((), ())), preferred_element_type=F32
        )

    def target_row(group):
        wanted = slot_id == group * CAP + lane_cap
        block = jnp.sum(jnp.where(wanted, m.spread_slots[...], 0.0), axis=0, keepdims=True)
        return block * 8.0 + feature

    targets((src // d.nx) * d.ncol + z * d.nx + lax.rem(src, d.nx))
    m.to_row[d.ny] = target_row(r)
    targets(y * d.na + src)

    for pos in range(d.ny):
        gy = lax.rem(y + offset_of(pos, d.ny) + d.ny, d.ny)
        m.to_row[pos] = target_row(gy * NK + k)
    dense_rows = d.blocks * 8
    row_id = lax.broadcasted_iota(jnp.int32, (dense_rows, d.na * 16), 0).astype(F32)

    def selector(at):
        return jnp.where(row_id == m.to_row[at], 1.0, 0.0).astype(BF)

    m.pick_b[...] = selector(d.ny)

    def keep_pick(pos):
        m.pick_a[pos] = selector(pos)

    each(0, d.ny, keep_pick)
    ring_a = Ring(d.ny, y, dense_rows, lambda j: (j * NK + k, c), m.send_ra, m.recv_ra, m.recv_ga)
    ring_b = Ring(d.nz, z, dense_rows, lambda j: (r, j * d.nx + x), m.send_rb, m.recv_rb, m.recv_gb)

    def aggregate_a(pos):
        m.dense_a[pos] = jnp.dot(
            m.pick_a[pos], m.got_a[pos], preferred_element_type=F32
        ).astype(BF)

    def aggregate_b(first, stop):
        lanes = slice(first * BLK, stop * BLK)
        total = jnp.dot(m.pick_b[...], m.got_b[:, lanes], preferred_element_type=F32).astype(BF)
        for pos in range(first, stop):
            m.dense_b[pos] = total[:, (pos - first) * BLK : (pos - first + 1) * BLK]

    def rings(last):
        for step in range(max(d.ny, d.nz) // 2):
            ring_b.reduce_step(step, m.dense_b, m.ring_got_b, m.stage_b, last)
            ring_a.reduce_step(step, m.dense_a, m.ring_got_a, m.stage_a, last)

    drain(m.got_b.at[:, pl.ds(0, far_b * BLK)], recv.at[2])
    aggregate_b(0, far_b)
    drain(m.got_a.at[pl.ds(0, far_a)], recv.at[1])
    each(0, far_a, aggregate_a)
    rings(False)
    drain(m.got_b.at[:, pl.ds(far_b * BLK, (d.nz - far_b) * BLK)], recv.at[3])
    aggregate_b(far_b, d.nz)
    drain(m.got_a.at[pl.ds(far_a, d.ny - far_a)], recv.at[12])
    each(far_a, d.ny, aggregate_a)
    rings(True)

    def widen_a(src, pos, piece):
        n = d.blocks // 2
        m.wide_a[pl.ds(pos * d.blocks + piece * n, n)] = (
            m.all_a[src, ring_a.rows(piece)].astype(F32).reshape(n, 8, BLK)
        )

    def widen_b(src, pos, piece):
        n = d.blocks // 2
        m.wide_b[pl.ds(pos * d.blocks + piece * n, n)] = (
            m.all_b[src, ring_b.rows(piece)].astype(F32).reshape(n, 8, BLK)
        )

    for piece in range(2):
        ends_b = ring_b.reduce_end(piece, m.ring_got_b)
        ends_a = ring_a.reduce_end(piece, m.ring_got_a)
        first = piece * d.blocks // 4

        def activate(p):
            rows = pl.ds(pl.multiple_of(p * 16, 16), 16)
            local = pl.ds(pl.multiple_of((p - first) * 16, 16), 16)
            sum_a = m.dense_a[d.ny - 1, rows].astype(F32)
            for at in ends_a:
                sum_a += m.ring_got_a[at, local].astype(F32)
            sum_b = m.dense_b[d.nz - 1, rows].astype(F32)
            for at in ends_b:
                sum_b += m.ring_got_b[at, local].astype(F32)
            low, high = [], []
            for part in range(2):
                pick = slice(part * 8, part * 8 + 8)
                pre = jnp.concatenate([sum_a[pick], sum_b[pick]], axis=0)
                lanes = pl.ds(pl.multiple_of((p * 2 + part) * BLK, BLK), BLK)
                sigma = jax.nn.sigmoid(pre)
                m.mixed[:, lanes] = (pre * sigma).astype(BF)
                grad = m.cotangent[:, lanes].astype(F32) * sigma * (1.0 + pre * (1.0 - sigma))
                low.append(grad[:8])
                high.append(grad[8:])
            m.all_a[y, rows] = jnp.concatenate(low, axis=0).astype(BF)
            m.all_b[z, rows] = jnp.concatenate(high, axis=0).astype(BF)

        each(first, first + d.blocks // 4, activate)
        ring_a.gather_step(0, piece, m.all_a, widen_a)
        ring_b.gather_step(0, piece, m.all_b, widen_b)
        widen_a(y, d.ny - 1, piece)
        widen_b(z, d.nz - 1, piece)

    def gathers(step):
        for piece in range(2):
            ring_a.gather_step(step, piece, m.all_a, widen_a)
            ring_b.gather_step(step, piece, m.all_b, widen_b)

    near_a, near_b = near_start(d.ny), near_start(d.nz)

    def columns(far):
        if far:
            return pl.ds(pl.multiple_of(k * d.ny * BLK, BLK), near_a * BLK)
        at = pl.multiple_of((k * d.ny + near_a) * BLK, BLK)
        return pl.ds(at, (d.ny - near_a) * BLK)

    def column(to_y):
        pos = pos_of(lax.rem(y - to_y + d.ny, d.ny), d.ny)
        return pl.ds(pl.multiple_of((k * d.ny + pos) * BLK, BLK), BLK)

    def message(i, far):
        to_k, to_col = peer_a(i)
        to_row, to_x = peer_b(i)
        a, b = to_k * d.ncol + to_col, to_row * d.nx + to_x
        first, stop = (0, near_a) if far else (near_a, d.ny)
        base = ((y * NK + to_k) * d.ncol + to_col) * d.slots + k * CAP
        for pos in range(first, stop):
            slot = base + group_slot[pos]
            rows = [
                m.wide_a[pos * d.blocks + m.slot_flat[slot + cap]] for cap in range(CAP)
            ]
            m.back_a[a, :, pos * BLK : (pos + 1) * BLK] = jnp.concatenate(rows, axis=0).astype(BF)
        src_a = m.back_a.at[a, :, pl.ds(first * BLK, (stop - first) * BLK)]
        dst_a = m.grads_a.at[pl.ds(pl.multiple_of(c * 16, 16), 16), columns(far)]
        first, stop = (0, near_b) if far else (near_b, d.nz)
        base = (to_row * d.ncol + z * d.nx + to_x) * d.slots
        at = [m.slot_flat[base + r * CAP + cap] for cap in range(CAP)]
        for pos in range(first, stop):
            rows = [m.wide_b[pos * d.blocks + at[cap]] for cap in range(CAP)]
            m.back_b[b, pos * 16 : pos * 16 + 16] = jnp.concatenate(rows, axis=0).astype(BF)
        src_b = m.back_b.at[b, pl.ds(first * 16, (stop - first) * 16)]
        to_rows = pl.ds(pl.multiple_of((x * d.nz + first) * 16, 16), (stop - first) * 16)
        dst_b = m.grads_b.at[to_rows, column(to_row // NK)]
        return src_a, dst_a, y * NK + to_k, to_col, src_b, dst_b, to_row, z * d.nx + to_x

    group_slot = [
        lax.rem(y + offset_of(pos, d.ny) + d.ny, d.ny) * NK * CAP for pos in range(d.ny)
    ]

    def give(far):
        sem_a, sem_b = (13, 14) if far else (4, 5)

        def run(i):
            src_a, dst_a, row_a, col_a, src_b, dst_b, row_b, col_b = message(i, far)
            remote(src_a, dst_a, send.at[sem_a], recv.at[sem_a], row_a, col_a).start()
            remote(src_b, dst_b, send.at[sem_b], recv.at[sem_b], row_b, col_b).start()

        return run

    def keep(far):
        sem_a, sem_b = (13, 14) if far else (4, 5)
        src_a, dst_a, _, _, src_b, dst_b, _, _ = message(0, far)
        pltpu.make_async_copy(src_a, dst_a, recv.at[sem_a]).start()
        pltpu.make_async_copy(src_b, dst_b, recv.at[sem_b]).start()

    top = max(d.ny, d.nz) // 2
    for step in range(1, min(2, top) + 1):
        gathers(step)
    each(1, d.na // 4, give(False))
    if top >= 3:
        gathers(3)
    each(d.na // 4, d.na // 2, give(False))
    if top >= 4:
        gathers(4)
    each(d.na // 2, d.na, give(False))
    each(1, d.na, give(True))
    keep(False)
    keep(True)

    span = d.ny * BLK
    drain(m.grads_a.at[:, pl.ds(0, NK * (d.ny - near_a) * BLK)], recv.at[4])
    for half_k in range(NK):
        lanes = slice(half_k * span + near_a * BLK, (half_k + 1) * span)
        value = jnp.dot(m.grads_a[:, lanes], m.matrix[lanes, :], preferred_element_type=F32)
        m.wide[0] = value if half_k == 0 else m.wide[0] + value
    drain(m.grads_b.at[pl.ds(0, d.nx * (d.nz - near_b) * 16)], recv.at[5])
    for to_x in range(d.nx):
        rows = slice((to_x * d.nz + near_b) * 16, (to_x + 1) * d.nz * 16)
        m.wide[1, rows] = jnp.dot(m.grads_b[rows], m.matrix[...], preferred_element_type=F32)
    drain(m.grads_a.at[:, pl.ds(0, NK * near_a * BLK)], recv.at[13])
    for half_k in range(NK):
        lanes = slice(half_k * span, half_k * span + near_a * BLK)
        m.wide[0] += jnp.dot(m.grads_a[:, lanes], m.matrix[lanes, :], preferred_element_type=F32)
    drain(m.grads_b.at[pl.ds(0, d.nx * near_b * 16)], recv.at[14])
    for to_x in range(d.nx):
        rows = slice(to_x * d.nz * 16, (to_x * d.nz + near_b) * 16)
        m.wide[1, rows] = jnp.dot(m.grads_b[rows], m.matrix[...], preferred_element_type=F32)

    def join(path):
        value = m.wide[path].reshape(d.ncol, CAP, 8, 4 * BLK)
        return value[:, 0, :, : 2 * BLK] + value[:, 1, :, 2 * BLK :]

    m.joined[:, 0] = join(0)
    high = join(1).reshape(d.nx, d.nz, 8, 256)
    for pos in range(d.nz):
        to_z = lax.rem(z + offset_of(pos, d.nz) + d.nz, d.nz)
        m.joined[pl.ds(to_z * d.nx, d.nx), 1] = high[:, pos]
    m.grad_y[...] = m.joined[...].reshape(d.width, 256).astype(BF)

    part = lax.dot_general(
        m.slab[...], m.grad_y[...], (((1,), (1,)), ((), ())), preferred_element_type=F32
    )
    m.parts[0] = part[:, :half]
    m.parts[1] = part[:, half:]
    twin_row = y * NK + (1 - k)
    swap = remote(m.parts.at[1 - k], m.twin, send.at[6], recv.at[6], twin_row, c)
    swap.start()
    m.grad_slab[...] = jnp.dot(
        m.weight[...], m.grad_y[...], preferred_element_type=F32
    ).astype(BF)
    swap.wait()
    m.summed[...] = (m.parts[k] + m.twin[...]).astype(BF)

    def rows_of(ref, col):
        return ref.at[pl.ds(pl.multiple_of(col * 16, 16), 16)]

    own_nodes = m.feat_grad.at[:, pl.ds(pl.multiple_of(c * 256, 256), 256)]
    pltpu.make_async_copy(rows_of(m.summed, c), m.spread.at[c], recv.at[7]).start()
    pltpu.make_async_copy(rows_of(m.grad_slab, c), own_nodes, recv.at[8]).start()

    def scatter(i):
        to = peer_col(i)
        remote(rows_of(m.summed, to), m.spread.at[c], send.at[7], recv.at[7], r, to).start()

    def features(i):
        to = peer_col(i)
        remote(rows_of(m.grad_slab, to), own_nodes, send.at[8], recv.at[8], r, to).start()

    each(1, d.ncol, scatter)
    each(1, d.ncol, features)
    drain(m.spread, recv.at[7])
    total = m.spread[0].astype(F32)
    for j in range(1, d.ncol):
        total += m.spread[j].astype(F32)
    m.mine[...] = total
    pltpu.make_async_copy(m.mine, m.rows_all.at[y], recv.at[9]).start()

    def along_y(i):
        to = lax.rem(y + i, d.ny)
        remote(m.mine, m.rows_all.at[y], send.at[9], recv.at[9], to * NK + k, c).start()

    each(1, d.ny, along_y)
    drain(m.rows_all, recv.at[9])
    total = m.rows_all[0]
    for j in range(1, d.ny):
        total += m.rows_all[j]
    m.final[...] = (total * scale).astype(BF)
    own_rows_w = m.whole.at[k, pl.ds(pl.multiple_of(c * 16, 16), 16)]
    pltpu.make_async_copy(m.final, own_rows_w, recv.at[10]).start()

    def publish(i):
        to = peer_col(i)
        remote(m.final, own_rows_w, send.at[10], recv.at[10], r, to).start()

    each(1, d.ncol, publish)
    drain(m.whole.at[k], recv.at[10])
    share = remote(m.whole.at[k], m.whole.at[k], send.at[11], recv.at[11], twin_row, c)
    share.start()
    share.wait()
    m.weight_grad[:, :half] = m.whole[0].astype(F32)
    m.weight_grad[:, half:] = m.whole[1].astype(F32)
    drain(m.slab.at[pl.ds(0, d.width - 16)], send.at[0])
    rest = pl.ds(0, d.na - 1)
    drain(m.out_a.at[rest, pl.ds(0, far_a)], send.at[1])
    drain(m.out_a.at[rest, pl.ds(far_a, d.ny - far_a)], send.at[12])
    drain(m.out_b.at[rest, :, pl.ds(0, far_b * BLK)], send.at[2])
    drain(m.out_b.at[rest, :, pl.ds(far_b * BLK, (d.nz - far_b) * BLK)], send.at[3])
    for ring, got, sem in ((ring_a, m.ring_got_a, m.send_ra), (ring_b, m.ring_got_b, m.send_rb)):
        for _ in range(2):
            drain(got.at[pl.ds(0, ring.copies())], sem.at[0])
    drain(m.back_a.at[rest, :, pl.ds(near_a * BLK, (d.ny - near_a) * BLK)], send.at[4])
    drain(m.back_a.at[rest, :, pl.ds(0, near_a * BLK)], send.at[13])
    drain(m.back_b.at[rest, pl.ds(near_b * 16, (d.nz - near_b) * 16)], send.at[5])
    drain(m.back_b.at[rest, pl.ds(0, near_b * 16)], send.at[14])
    drain(m.spread.at[pl.ds(0, d.ncol - 1)], send.at[7])
    drain(m.grad_slab.at[pl.ds(0, d.width - 16)], send.at[8])
    drain(m.rows_all.at[pl.ds(0, d.ny - 1)], send.at[9])
    drain(m.whole.at[0, pl.ds(0, d.width - 16)], send.at[10])
    drain(m.grad_slab, recv.at[8])


def body(d, node_total, feats, weight, tile_vals, tile_src, tile_slot, slot_block, cotangent):
    vmem = pl.BlockSpec(memory_space=pltpu.VMEM)
    smem = pl.BlockSpec(memory_space=pltpu.SMEM)
    anywhere = pl.BlockSpec(memory_space=pl.ANY)
    sds = jax.ShapeDtypeStruct
    pair = tile_slot[0] * 2 + tile_src[0]
    pair_ids = jnp.arange(2 * d.slots, dtype=jnp.int32)
    tile_ids = jnp.arange(tile_vals.shape[0], dtype=jnp.int32)
    inv = jnp.max(jnp.where(pair[:, None] == pair_ids[None, :], tile_ids[:, None], -1), axis=0)
    inputs = dict(
        inv=(inv, smem),
        slot_flat=(slot_block.reshape(-1), smem),
        slot_table=(slot_block, vmem),
        feats=(feats, vmem),
        weight=(weight, vmem),
        tiles=(tile_vals, vmem),
        cotangent=(cotangent, vmem),
    )
    outputs = dict(
        mixed=(sds(cotangent.shape, BF), vmem),
        feat_grad=(sds(feats.shape, BF), anywhere),
        weight_grad=(sds((d.width, d.width), F32), vmem),
    )
    half, dense_rows, hops_a, hops_b = d.width // 2, d.blocks * 8, max(1, d.ny // 2), max(1, d.nz // 2)
    dma = pltpu.SemaphoreType.DMA
    scratch = dict(
        slab=((d.width, 256), BF),
        weight_t=((d.width, d.width), BF),
        proj=((d.width, 256), BF),
        matrix=((d.nrow * BLK, 4 * BLK), BF),
        out_a=((d.na, d.ny, 16, BLK), BF),
        out_b=((d.nb, 16, d.nz * BLK), BF),
        got_a=((d.ny, d.na * 16, BLK), BF),
        got_b=((d.nb * 16, d.nz * BLK), BF),
        spread_slots=((d.slots, d.na * 16), F32),
        to_row=((d.ny + 1, 1, d.na * 16), F32),
        joined=((d.ncol, 2, 8, 256), F32),
        pick_a=((d.ny, dense_rows, d.na * 16), BF),
        pick_b=((dense_rows, d.nb * 16), BF),
        dense_a=((d.ny, dense_rows, BLK), BF),
        dense_b=((d.nz, dense_rows, BLK), BF),
        ring_got_a=((4 * hops_a, dense_rows // 2, BLK), BF),
        ring_got_b=((4 * hops_b, dense_rows // 2, BLK), BF),
        stage_a=((4 * hops_a, dense_rows // 2, BLK), BF),
        stage_b=((4 * hops_b, dense_rows // 2, BLK), BF),
        all_a=((d.ny, dense_rows, BLK), BF),
        all_b=((d.nz, dense_rows, BLK), BF),
        wide_a=((d.ny * d.blocks, 8, BLK), F32),
        wide_b=((d.nz * d.blocks, 8, BLK), F32),
        back_a=((d.na, 16, d.ny * BLK), BF),
        back_b=((d.nb, d.nz * 16, BLK), BF),
        grads_a=((d.width, d.nrow * BLK), BF),
        grads_b=((d.width, d.nrow * BLK), BF),
        wide=((2, d.width, 4 * BLK), F32),
        grad_y=((d.width, 256), BF),
        grad_slab=((d.width, 256), BF),
        parts=((2, d.width, half), F32),
        twin=((d.width, half), F32),
        summed=((d.width, half), BF),
        spread=((d.ncol, 16, half), BF),
        mine=((16, half), F32),
        rows_all=((d.ny, 16, half), F32),
        final=((16, half), BF),
        whole=((2, d.width, half), BF),
    )
    semaphores = dict(
        send=15, recv=15, send_ra=1, send_rb=1, recv_ra=4 * hops_a, recv_rb=4 * hops_b
    )
    semaphores.update(recv_ga=4 * hops_a, recv_gb=4 * hops_b)
    names = tuple(inputs) + tuple(outputs) + tuple(scratch) + tuple(semaphores)
    return pl.pallas_call(
        functools.partial(whole_kernel, d, 1.0 / math.sqrt(node_total), names),
        out_shape=tuple(v[0] for v in outputs.values()),
        in_specs=[v[1] for v in inputs.values()],
        out_specs=tuple(v[1] for v in outputs.values()),
        scratch_shapes=[pltpu.VMEM(*v) for v in scratch.values()]
        + [dma((n,)) for n in semaphores.values()],
        compiler_params=pltpu.CompilerParams(
            collective_id=0, has_side_effects=True, vmem_limit_bytes=LIMIT
        ),
        name="layer",
    )(*(v[0] for v in inputs.values()))


def solution(mesh):
    d = Dims(mesh.shape["row"], mesh.shape["col"])
    placed = (
        P("col", "row"),
        P(),
        P(("row", "col"), None, None),
        P(("row", "col"), None),
        P(("row", "col"), None),
        P(),
        P("col", "row"),
    )
    node_total = d.nrow * d.ncol * 2 * BLK
    return jax.shard_map(
        functools.partial(body, d, node_total),
        mesh=mesh,
        in_specs=placed,
        out_specs=(P("col", "row"), P("col", "row"), P()),
        check_vma=False,
    )
```

```python
import functools
import math
import types

import jax
import jax.numpy as jnp
from jax import lax
from jax.experimental import pallas as pl
from jax.experimental.pallas import tpu as pltpu
from jax.sharding import PartitionSpec as P

BF = jnp.bfloat16
F32 = jnp.float32
MESH = pl.DeviceIdType.MESH
NK = 2
CAP = 2
BLK = 128
LIMIT = 56 * 1024 * 1024


class Dims:
    def __init__(self, n_row, n_col):
        self.nrow, self.ncol = n_row, n_col
        self.nx = 4 if n_col > 4 else 2
        self.ny, self.nz = n_row // NK, n_col // self.nx
        self.width = 16 * n_col
        self.blocks = 2 * n_col
        self.slots = CAP * n_row
        self.na = NK * n_col
        self.nb = n_row * self.nx
        self.ncol_b = self.nb // NK
        self.slot_devices = n_row * n_col
        assert self.na == self.nb

    def here(self):
        r, c = lax.axis_index("row"), lax.axis_index("col")
        return r, c, r // NK, lax.rem(r, NK), c // self.nx, lax.rem(c, self.nx)


def remote(src, dst, send_sem, recv_sem, row, col):
    return pltpu.make_async_remote_copy(
        src_ref=src,
        dst_ref=dst,
        send_sem=send_sem,
        recv_sem=recv_sem,
        device_id=(row, col),
        device_id_type=MESH,
    )


def drain(ref, sem):
    pltpu.make_async_copy(ref, ref, sem).wait()


def each(start, stop, step):
    def run(i, carry):
        step(i)
        return carry

    lax.fori_loop(start, stop, run, 0)


def greet(barrier, row, col):
    pl.semaphore_signal(barrier, inc=1, device_id=(row, col), device_id_type=MESH)


def tile_of(inv, tiles, group, cap, source):
    at = inv[(group * CAP + cap) * 2 + source]
    value = tiles[jnp.maximum(at, 0)]
    return jnp.where(at >= 0, value, jnp.zeros_like(value))


def ways(n, way, piece):
    return n // 2 if way == piece else (n - 1) // 2


def offset_of(pos, n):
    if pos == 0:
        return n // 2
    return n // 2 - (pos + 1) // 2 if pos % 2 else -(n // 2 - pos // 2)


def pos_of(offset, n):
    if isinstance(offset, int):
        return [p for p in range(n) if (offset_of(p, n) - offset) % n == 0][0]
    return jnp.where(offset > n // 2, 2 * offset - n, jnp.maximum(n - 1 - 2 * offset, 0))


def far_count(n):
    return max(1, n - 3)


def near_start(n):
    return max(1, n - 3)


class Ring:
    def __init__(self, n, me, rows, device, send, recv, recv_gather):
        self.n, self.me, self.half, self.device = n, me, rows // 2, device
        self.send, self.recv, self.recv_gather = send, recv, recv_gather
        self.hops = max(1, n // 2)

    def at(self, way, piece, step):
        return (way * 2 + piece) * self.hops + step

    def rows(self, piece):
        return pl.ds(piece * self.half, self.half)

    def near(self, offset):
        return lax.rem(self.me + offset + self.n, self.n)

    def copies(self):
        return sum(ways(self.n, w, p) for w in range(2) for p in range(2))

    def start(self, src, dst, way, piece, step, recv):
        row, col = self.device(self.near(1 - 2 * way))
        at = self.at(way, piece, step)
        remote(src, dst, self.send.at[0], recv.at[at], row, col).start()

    def reduce_step(self, step, dense, got, stage, last):
        for piece in range(2):
            for way in range(2):
                hops = ways(self.n, way, piece)
                if step >= hops:
                    continue
                to = pos_of((1 - 2 * way) * (hops - step), self.n)
                if (to >= far_count(self.n)) != last:
                    continue
                if step == 0:
                    src = dense.at[to, self.rows(piece)]
                else:
                    old = self.at(way, piece, step - 1)
                    drain(got.at[old], self.recv.at[old])
                    new = self.at(way, piece, step)
                    total = got[old].astype(F32) + dense[to, self.rows(piece)].astype(F32)
                    stage[new] = total.astype(BF)
                    src = stage.at[new]
                self.start(src, got.at[self.at(way, piece, step)], way, piece, step, self.recv)

    def reduce_end(self, piece, got):
        ends = []
        for way in range(2):
            hops = ways(self.n, way, piece)
            if hops:
                at = self.at(way, piece, hops - 1)
                drain(got.at[at], self.recv.at[at])
                ends.append(at)
        return ends

    def gather_step(self, step, piece, held, widen):
        for way in range(2):
            hops = ways(self.n, way, piece)
            if step > hops or hops == 0:
                continue
            src = self.near(-(1 - 2 * way) * step)
            pos = pos_of(-(1 - 2 * way) * step, self.n)
            part = held.at[src, self.rows(piece)]
            if step:
                drain(part, self.recv_gather.at[self.at(way, piece, step - 1)])
            if step < hops:
                self.start(part, part, way, piece, step, self.recv_gather)
            if step:
                widen(src, pos, piece)


def whole_kernel(d, scale, names, *refs):
    m = types.SimpleNamespace(**dict(zip(names, refs)))
    r, c, y, k, z, x = d.here()
    me_a, me_b = k * d.ncol + c, r * d.nx + x
    half = d.width // 2
    send, recv = m.send, m.recv
    barrier = pltpu.get_barrier_semaphore()

    def turn(i, n):
        j = (i + 1) // 2
        return jnp.where(lax.rem(i, 2) == 1, j, lax.rem(n - j, n))

    x_of = [lax.rem(x + j, d.nx) for j in range(d.nx)]
    k_of = [k, 1 - k]

    def line_a(other, jz, visit):
        first = isinstance(jz, int)
        to_z = z if first else lax.rem(z + turn(jz, d.nz), d.nz)
        for j in range(1 if first and not other else 0, d.nx):
            visit(y * NK + k_of[other], to_z * d.nx + x_of[j], k_of[other])

    def line_b(other, jy, visit):
        first = isinstance(jy, int)
        to_y = y if first else lax.rem(y + turn(jy, d.ny), d.ny)
        for j in range(1 if first and not other else 0, d.nx):
            visit(to_y * NK + k_of[other], z * d.nx + x_of[j], to_y, x_of[j])

    def peers_a(other, visit):
        line_a(other, 0, visit)
        each(1, d.nz, lambda jz: line_a(other, jz, visit))

    def peers_b(other, visit):
        line_b(other, 0, visit)
        each(1, d.ny, lambda jy: line_b(other, jy, visit))

    loads = [
        pltpu.make_async_copy(src, dst, m.load.at[at])
        for at, (src, dst) in enumerate(
            (
                (m.tiles_in, m.tiles),
                (m.weight_in, m.weight),
                (m.slot_table_in, m.slot_table),
                (m.cotangent_in, m.cotangent),
            )
        )
    ]
    for load in loads:
        load.start()
    for other in range(NK):
        peers_a(other, lambda row, col, _: greet(barrier, row, col))
        peers_b(other, lambda row, col, *_: greet(barrier, row, col))

    def place(group):
        offset = lax.rem(group // NK - y + d.ny, d.ny)
        at = pl.multiple_of((lax.rem(group, NK) * d.ny + pos_of(offset, d.ny)) * BLK, BLK)
        for cap in range(CAP):
            for s in range(2):
                lanes = slice((cap * 2 + s) * BLK, (cap * 2 + s + 1) * BLK)
                m.matrix[pl.ds(at, BLK), lanes] = tile_of(m.inv, m.tiles, group, cap, s)

    pl.semaphore_wait(barrier, d.na - 1 + d.nb - 1)

    def nodes_of(col):
        return m.feats.at[:, pl.ds(pl.multiple_of(col * 256, 256), 256)]

    own_rows = m.slab.at[pl.ds(pl.multiple_of(c * 16, 16), 16)]
    pltpu.make_async_copy(nodes_of(c), own_rows, recv.at[0]).start()

    def send_feats(row, col, _):
        remote(nodes_of(col), own_rows, send.at[0], recv.at[0], row, col).start()

    peers_a(0, send_feats)
    loads[0].wait()
    each(0, d.nrow, place)
    loads[1].wait()
    m.weight_t[...] = m.weight[...].T
    drain(m.slab, recv.at[0])
    value = jnp.dot(m.weight_t[...], m.slab[...], preferred_element_type=F32)
    value = value.reshape(d.ncol, 2, 8, 256)
    value = jnp.concatenate([value[:, 0], value[:, 1]], axis=0)
    m.proj[...] = value.reshape(d.width, 256).astype(BF)

    far_a, far_b = far_count(d.ny), far_count(d.nz)
    lanes_of = [
        pl.ds(pl.multiple_of(pos_of(lax.rem(j - z + d.nz, d.nz), d.nz) * BLK, BLK), BLK)
        for j in range(d.nz)
    ]

    def send_b(group, late):
        lanes = pl.ds(far_b * BLK, (d.nz - far_b) * BLK) if late else pl.ds(0, far_b * BLK)
        sem = 3 if late else 2

        def send_to(to_x):
            src = m.out_b.at[group * d.nx + to_x, :, lanes]
            dst = m.got_b.at[pl.ds(pl.multiple_of(me_b * 16, 16), 16), lanes]
            remote(src, dst, send.at[sem], recv.at[sem], group, z * d.nx + to_x).start()

        @pl.when(group != r)
        def _():
            send_to(x)

        for j in range(1, d.nx):
            send_to(x_of[j])

    def group_step(gk, pos):
        gy = lax.rem(y + offset_of(pos, d.ny) + d.ny, d.ny)
        group = gy * NK + gk
        at = pl.multiple_of((gk * d.ny + pos) * BLK, BLK)
        both = jnp.concatenate(
            [m.matrix[pl.ds(at, BLK), : 2 * BLK], m.matrix[pl.ds(at, BLK), 2 * BLK :]], axis=0
        )
        part = lax.dot_general(
            m.proj[...], both, (((1,), (1,)), ((), ())), preferred_element_type=F32
        )
        first = part[:, :BLK].reshape(2 * d.ncol, 8, BLK)
        second = part[:, BLK:].reshape(2 * d.ncol, 8, BLK)
        packed = jnp.concatenate([first, second], axis=1).astype(BF)
        m.out_a[pl.ds(gk * d.ncol, d.ncol), pos] = packed[: d.ncol]
        for to_x in range(d.nx):
            for to_z in range(d.nz):
                m.out_b[group * d.nx + to_x, :, lanes_of[to_z]] = packed[
                    d.ncol + to_z * d.nx + to_x
                ]
        send_b(group, False)

    def send_a(late):
        part = pl.ds(far_a, d.ny - far_a) if late else pl.ds(0, far_a)
        sem = 12 if late else 1
        dst = m.got_a.at[part, pl.ds(pl.multiple_of(me_a * 16, 16), 16)]

        def visit(row, col, to_k):
            src = m.out_a.at[to_k * d.ncol + col, part]
            remote(src, dst, send.at[sem], recv.at[sem], row, col).start()

        return visit

    for late in range(2):
        for first_k in range(2):
            gk = k if first_k == 0 else 1 - k
            for pos in range(far_a, d.ny) if late else range(far_a):
                group_step(gk, pos)
            if not late:
                peers_a(first_k, send_a(False))
    each(0, d.nrow, lambda i: send_b(lax.rem(r + i, d.nrow), True))
    for other in range(NK):
        peers_a(other, send_a(True))
    for late in range(2):
        part = pl.ds(far_a, d.ny - far_a) if late else pl.ds(0, far_a)
        pltpu.make_async_copy(
            m.out_a.at[me_a, part],
            m.got_a.at[part, pl.ds(pl.multiple_of(me_a * 16, 16), 16)],
            recv.at[12 if late else 1],
        ).start()
        lanes = pl.ds(far_b * BLK, (d.nz - far_b) * BLK) if late else pl.ds(0, far_b * BLK)
        pltpu.make_async_copy(
            m.out_b.at[me_b, :, lanes],
            m.got_b.at[pl.ds(pl.multiple_of(me_b * 16, 16), 16), lanes],
            recv.at[3 if late else 2],
        ).start()

    lane = lax.broadcasted_iota(jnp.int32, (d.slot_devices, d.na * 16), 1)
    device = lax.broadcasted_iota(jnp.int32, (d.slot_devices, d.na * 16), 0)
    src = lane // 16
    loads[2].wait()
    table = m.slot_table[...].astype(F32).astype(BF)
    row_lane = lax.broadcasted_iota(jnp.int32, (1, d.na * 16), 1)
    slot_id = lax.broadcasted_iota(jnp.int32, (d.slots, d.na * 16), 0)
    slot_lane = lax.broadcasted_iota(jnp.int32, (d.slots, d.na * 16), 1)
    lane_cap = lax.rem(slot_lane, 16) // 8
    feature = lax.rem(row_lane, 8).astype(F32)

    def targets(owner):
        onehot = jnp.where(device == owner, 1.0, 0.0).astype(BF)
        m.spread_slots[...] = lax.dot_general(
            table, onehot, (((1,), (0,)), ((), ())), preferred_element_type=F32
        )

    def target_row(group):
        wanted = slot_id == group * CAP + lane_cap
        block = jnp.sum(jnp.where(wanted, m.spread_slots[...], 0.0), axis=0, keepdims=True)
        return block * 8.0 + feature

    targets((src // d.nx) * d.ncol + z * d.nx + lax.rem(src, d.nx))
    m.to_row[d.ny] = target_row(r)
    targets(y * d.na + src)

    for pos in range(d.ny):
        gy = lax.rem(y + offset_of(pos, d.ny) + d.ny, d.ny)
        m.to_row[pos] = target_row(gy * NK + k)
    dense_rows = d.blocks * 8
    row_id = lax.broadcasted_iota(jnp.int32, (dense_rows, d.na * 16), 0).astype(F32)

    def selector(at):
        return jnp.where(row_id == m.to_row[at], 1.0, 0.0).astype(BF)

    m.pick_b[...] = selector(d.ny)

    def keep_pick(pos):
        m.pick_a[pos] = selector(pos)

    each(0, d.ny, keep_pick)
    ring_a = Ring(d.ny, y, dense_rows, lambda j: (j * NK + k, c), m.send_ra, m.recv_ra, m.recv_ga)
    ring_b = Ring(d.nz, z, dense_rows, lambda j: (r, j * d.nx + x), m.send_rb, m.recv_rb, m.recv_gb)

    def aggregate_a(pos):
        m.dense_a[pos] = jnp.dot(
            m.pick_a[pos], m.got_a[pos], preferred_element_type=F32
        ).astype(BF)

    def aggregate_b(first, stop):
        lanes = slice(first * BLK, stop * BLK)
        total = jnp.dot(m.pick_b[...], m.got_b[:, lanes], preferred_element_type=F32).astype(BF)
        for pos in range(first, stop):
            m.dense_b[pos] = total[:, (pos - first) * BLK : (pos - first + 1) * BLK]

    def rings(last):
        for step in range(max(d.ny, d.nz) // 2):
            ring_b.reduce_step(step, m.dense_b, m.ring_got_b, m.stage_b, last)
            ring_a.reduce_step(step, m.dense_a, m.ring_got_a, m.stage_a, last)

    drain(m.got_b.at[:, pl.ds(0, far_b * BLK)], recv.at[2])
    aggregate_b(0, far_b)
    drain(m.got_a.at[pl.ds(0, far_a)], recv.at[1])
    each(0, far_a, aggregate_a)
    rings(False)
    drain(m.got_b.at[:, pl.ds(far_b * BLK, (d.nz - far_b) * BLK)], recv.at[3])
    aggregate_b(far_b, d.nz)
    drain(m.got_a.at[pl.ds(far_a, d.ny - far_a)], recv.at[12])
    each(far_a, d.ny, aggregate_a)
    rings(True)
    loads[3].wait()

    def widen_a(src, pos, piece):
        n = d.blocks // 2
        m.wide_a[pl.ds(pos * d.blocks + piece * n, n)] = (
            m.all_a[src, ring_a.rows(piece)].astype(F32).reshape(n, 8, BLK)
        )

    def widen_b(src, pos, piece):
        n = d.blocks // 2
        m.wide_b[pl.ds(pos * d.blocks + piece * n, n)] = (
            m.all_b[src, ring_b.rows(piece)].astype(F32).reshape(n, 8, BLK)
        )

    for piece in range(2):
        ends_b = ring_b.reduce_end(piece, m.ring_got_b)
        ends_a = ring_a.reduce_end(piece, m.ring_got_a)
        first = piece * d.blocks // 4

        def activate(p):
            rows = pl.ds(pl.multiple_of(p * 16, 16), 16)
            local = pl.ds(pl.multiple_of((p - first) * 16, 16), 16)
            sum_a = m.dense_a[d.ny - 1, rows].astype(F32)
            for at in ends_a:
                sum_a += m.ring_got_a[at, local].astype(F32)
            sum_b = m.dense_b[d.nz - 1, rows].astype(F32)
            for at in ends_b:
                sum_b += m.ring_got_b[at, local].astype(F32)
            low, high = [], []
            for part in range(2):
                pick = slice(part * 8, part * 8 + 8)
                pre = jnp.concatenate([sum_a[pick], sum_b[pick]], axis=0)
                lanes = pl.ds(pl.multiple_of((p * 2 + part) * BLK, BLK), BLK)
                sigma = jax.nn.sigmoid(pre)
                m.mixed[:, lanes] = (pre * sigma).astype(BF)
                grad = m.cotangent[:, lanes].astype(F32) * sigma * (1.0 + pre * (1.0 - sigma))
                low.append(grad[:8])
                high.append(grad[8:])
            m.all_a[y, rows] = jnp.concatenate(low, axis=0).astype(BF)
            m.all_b[z, rows] = jnp.concatenate(high, axis=0).astype(BF)

        each(first, first + d.blocks // 4, activate)
        ring_a.gather_step(0, piece, m.all_a, widen_a)
        ring_b.gather_step(0, piece, m.all_b, widen_b)
        widen_a(y, d.ny - 1, piece)
        widen_b(z, d.nz - 1, piece)

    def gathers(step):
        for piece in range(2):
            ring_a.gather_step(step, piece, m.all_a, widen_a)
            ring_b.gather_step(step, piece, m.all_b, widen_b)

    near_a, near_b = near_start(d.ny), near_start(d.nz)

    def columns(far):
        if far:
            return pl.ds(pl.multiple_of(k * d.ny * BLK, BLK), near_a * BLK)
        at = pl.multiple_of((k * d.ny + near_a) * BLK, BLK)
        return pl.ds(at, (d.ny - near_a) * BLK)

    def column(to_y):
        pos = pos_of(lax.rem(y - to_y + d.ny, d.ny), d.ny)
        return pl.ds(pl.multiple_of((k * d.ny + pos) * BLK, BLK), BLK)

    group_slot = [
        (lax.rem(y + offset_of(pos, d.ny) + d.ny, d.ny) * NK + k) * CAP for pos in range(d.ny)
    ]

    def give_a(far, row, col, to_k):
        first, stop = (0, near_a) if far else (near_a, d.ny)
        a, device = to_k * d.ncol + col, row * d.ncol + col
        for pos in range(first, stop):
            rows = [
                m.wide_a[pos * d.blocks + m.slots[group_slot[pos] + cap, device]]
                for cap in range(CAP)
            ]
            m.back_a[a, :, pos * BLK : (pos + 1) * BLK] = jnp.concatenate(rows, axis=0).astype(BF)
        src = m.back_a.at[a, :, pl.ds(first * BLK, (stop - first) * BLK)]
        return src, m.grads_a.at[pl.ds(pl.multiple_of(c * 16, 16), 16), columns(far)]

    def give_b(far, row, col, to_y, to_x):
        first, stop = (0, near_b) if far else (near_b, d.nz)
        b, device = row * d.nx + to_x, row * d.ncol + col
        at = [m.slots[r * CAP + cap, device] for cap in range(CAP)]
        for pos in range(first, stop):
            rows = [m.wide_b[pos * d.blocks + at[cap]] for cap in range(CAP)]
            m.back_b[b, pos * 16 : pos * 16 + 16] = jnp.concatenate(rows, axis=0).astype(BF)
        src = m.back_b.at[b, pl.ds(first * 16, (stop - first) * 16)]
        to_rows = pl.ds(pl.multiple_of((x * d.nz + first) * 16, 16), (stop - first) * 16)
        return src, m.grads_b.at[to_rows, column(to_y)]

    def give(far, other, start, stop):
        sem_a, sem_b = (13, 14) if far else (4, 5)

        def visit_a(row, col, to_k):
            src, dst = give_a(far, row, col, to_k)
            remote(src, dst, send.at[sem_a], recv.at[sem_a], row, col).start()

        def visit_b(row, col, to_y, to_x):
            src, dst = give_b(far, row, col, to_y, to_x)
            remote(src, dst, send.at[sem_b], recv.at[sem_b], row, col).start()

        def both_lines(j):
            line_a(other, j, visit_a)
            line_b(other, j, visit_b)

        if start == 0:
            both_lines(0)
        each(max(1, start), stop, both_lines)

    def keep(far):
        sem_a, sem_b = (13, 14) if far else (4, 5)
        src, dst = give_a(far, r, c, k)
        pltpu.make_async_copy(src, dst, recv.at[sem_a]).start()
        src, dst = give_b(far, r, c, y, x)
        pltpu.make_async_copy(src, dst, recv.at[sem_b]).start()

    top, mid = max(d.ny, d.nz) // 2, d.ny // 2
    gathers(1)
    give(False, 0, 0, mid)
    if top >= 2:
        gathers(2)
    give(False, 0, mid, d.ny)
    if top >= 3:
        gathers(3)
    give(False, 1, 0, mid)
    if top >= 4:
        gathers(4)
    give(False, 1, mid, d.ny)
    give(True, 0, 0, d.ny)
    give(True, 1, 0, d.ny)
    keep(False)
    keep(True)

    span = d.ny * BLK
    drain(m.grads_a.at[:, pl.ds(0, NK * (d.ny - near_a) * BLK)], recv.at[4])
    for half_k in range(NK):
        lanes = slice(half_k * span + near_a * BLK, (half_k + 1) * span)
        value = jnp.dot(m.grads_a[:, lanes], m.matrix[lanes, :], preferred_element_type=F32)
        m.wide[0] = value if half_k == 0 else m.wide[0] + value
    drain(m.grads_b.at[pl.ds(0, d.nx * (d.nz - near_b) * 16)], recv.at[5])
    for to_x in range(d.nx):
        rows = slice((to_x * d.nz + near_b) * 16, (to_x + 1) * d.nz * 16)
        m.wide[1, rows] = jnp.dot(m.grads_b[rows], m.matrix[...], preferred_element_type=F32)
    drain(m.grads_a.at[:, pl.ds(0, NK * near_a * BLK)], recv.at[13])
    for half_k in range(NK):
        lanes = slice(half_k * span, half_k * span + near_a * BLK)
        m.wide[0] += jnp.dot(m.grads_a[:, lanes], m.matrix[lanes, :], preferred_element_type=F32)
    drain(m.grads_b.at[pl.ds(0, d.nx * near_b * 16)], recv.at[14])
    for to_x in range(d.nx):
        rows = slice(to_x * d.nz * 16, (to_x * d.nz + near_b) * 16)
        m.wide[1, rows] = jnp.dot(m.grads_b[rows], m.matrix[...], preferred_element_type=F32)

    def join(path):
        value = m.wide[path].reshape(d.ncol, CAP, 8, 4 * BLK)
        return value[:, 0, :, : 2 * BLK] + value[:, 1, :, 2 * BLK :]

    m.joined[:, 0] = join(0)
    high = join(1).reshape(d.nx, d.nz, 8, 256)
    for pos in range(d.nz):
        to_z = lax.rem(z + offset_of(pos, d.nz) + d.nz, d.nz)
        m.joined[pl.ds(to_z * d.nx, d.nx), 1] = high[:, pos]
    m.grad_y[...] = m.joined[...].reshape(d.width, 256).astype(BF)

    part = lax.dot_general(
        m.slab[...], m.grad_y[...], (((1,), (1,)), ((), ())), preferred_element_type=F32
    )
    m.parts[0] = part[:, :half]
    m.parts[1] = part[:, half:]
    m.to_twin[...] = m.parts[1 - k].astype(BF)
    twin_row = y * NK + (1 - k)
    swap = remote(m.to_twin, m.twin, send.at[6], recv.at[6], twin_row, c)
    swap.start()
    m.grad_slab[...] = jnp.dot(
        m.weight[...], m.grad_y[...], preferred_element_type=F32
    ).astype(BF)
    swap.wait()
    m.summed[...] = (m.parts[k] + m.twin[...].astype(F32)).astype(BF)

    def rows_of(ref, at):
        return ref.at[pl.ds(pl.multiple_of(at * 16, 16), 16)]

    me_w = y * d.nx + x
    own_nodes = m.feat_grad.at[:, pl.ds(pl.multiple_of(c * 256, 256), 256)]
    pltpu.make_async_copy(rows_of(m.summed, me_w), m.spread.at[me_w], recv.at[7]).start()
    pltpu.make_async_copy(rows_of(m.grad_slab, c), own_nodes, recv.at[8]).start()

    def scatter(row, col, to_y, to_x):
        src = rows_of(m.summed, to_y * d.nx + to_x)
        remote(src, m.spread.at[me_w], send.at[7], recv.at[7], row, col).start()

    def features(row, col, _):
        remote(rows_of(m.grad_slab, col), own_nodes, send.at[8], recv.at[8], row, col).start()

    peers_b(0, scatter)
    peers_a(0, features)
    drain(m.spread, recv.at[7])
    total = m.spread[0].astype(F32)
    for j in range(1, d.ncol_b):
        total += m.spread[j].astype(F32)
    m.mine[...] = total
    pltpu.make_async_copy(m.mine, m.rows_all.at[z], recv.at[9]).start()

    def along_z(i):
        to = lax.rem(z + i, d.nz)
        remote(m.mine, m.rows_all.at[z], send.at[9], recv.at[9], r, to * d.nx + x).start()

    each(1, d.nz, along_z)
    drain(m.rows_all, recv.at[9])
    total = m.rows_all[0]
    for j in range(1, d.nz):
        total += m.rows_all[j]
    m.final[...] = (total * scale).astype(BF)
    own_rows_w = m.whole.at[k, pl.ds(pl.multiple_of(me_w * 16, 16), 16)]
    pltpu.make_async_copy(m.final, own_rows_w, recv.at[10]).start()

    def publish(row, col, to_y, to_x):
        remote(m.final, own_rows_w, send.at[10], recv.at[10], row, col).start()

    peers_b(0, publish)
    drain(m.whole.at[k], recv.at[10])
    share = remote(m.whole.at[k], m.whole.at[k], send.at[11], recv.at[11], twin_row, c)
    share.start()
    share.wait()
    m.weight_raw[...] = m.whole[...]
    drain(m.slab.at[pl.ds(0, d.width - 16)], send.at[0])
    rest = pl.ds(0, d.na - 1)
    drain(m.out_a.at[rest, pl.ds(0, far_a)], send.at[1])
    drain(m.out_a.at[rest, pl.ds(far_a, d.ny - far_a)], send.at[12])
    drain(m.out_b.at[rest, :, pl.ds(0, far_b * BLK)], send.at[2])
    drain(m.out_b.at[rest, :, pl.ds(far_b * BLK, (d.nz - far_b) * BLK)], send.at[3])
    for ring, got, sem in ((ring_a, m.ring_got_a, m.send_ra), (ring_b, m.ring_got_b, m.send_rb)):
        for _ in range(2):
            drain(got.at[pl.ds(0, ring.copies())], sem.at[0])
    drain(m.back_a.at[rest, :, pl.ds(near_a * BLK, (d.ny - near_a) * BLK)], send.at[4])
    drain(m.back_a.at[rest, :, pl.ds(0, near_a * BLK)], send.at[13])
    drain(m.back_b.at[rest, pl.ds(near_b * 16, (d.nz - near_b) * 16)], send.at[5])
    drain(m.back_b.at[rest, pl.ds(0, near_b * 16)], send.at[14])
    drain(m.spread.at[pl.ds(0, d.ncol_b - 1)], send.at[7])
    drain(m.grad_slab.at[pl.ds(0, d.width - 16)], send.at[8])
    drain(m.rows_all.at[pl.ds(0, d.nz - 1)], send.at[9])
    drain(m.whole.at[0, pl.ds(0, d.width - 16)], send.at[10])
    drain(m.grad_slab, recv.at[8])


def finish_kernel(mixed_in, feat_in, weight_in, mixed, feat_grad, weight_grad):
    half = weight_in.shape[2]
    mixed[...] = mixed_in[...]
    feat_grad[...] = feat_in[...]
    weight_grad[:, :half] = weight_in[0].astype(F32)
    weight_grad[:, half:] = weight_in[1].astype(F32)


def body(d, node_total, feats, weight, tile_vals, tile_src, tile_slot, slot_block, cotangent):
    vmem = pl.BlockSpec(memory_space=pltpu.VMEM)
    smem = pl.BlockSpec(memory_space=pltpu.SMEM)
    anywhere = pl.BlockSpec(memory_space=pl.ANY)
    sds = jax.ShapeDtypeStruct
    pair = tile_slot[0] * 2 + tile_src[0]
    pair_ids = jnp.arange(2 * d.slots, dtype=jnp.int32)
    tile_ids = jnp.arange(tile_vals.shape[0], dtype=jnp.int32)
    inv = jnp.max(jnp.where(pair[:, None] == pair_ids[None, :], tile_ids[:, None], -1), axis=0)
    inputs = dict(
        inv=(inv, smem),
        slots=(slot_block.T, smem),
        slot_table_in=(slot_block.T, anywhere),
        feats=(feats, anywhere),
        weight_in=(weight, anywhere),
        tiles_in=(tile_vals, anywhere),
        cotangent_in=(cotangent, anywhere),
    )
    outputs = dict(
        mixed=(sds(cotangent.shape, BF), vmem),
        feat_grad=(sds(feats.shape, BF), anywhere),
        weight_raw=(sds((2, d.width, d.width // 2), BF), vmem),
    )
    half, dense_rows, hops_a, hops_b = d.width // 2, d.blocks * 8, max(1, d.ny // 2), max(1, d.nz // 2)
    dma = pltpu.SemaphoreType.DMA
    scratch = dict(
        tiles=(tile_vals.shape, BF),
        weight=((d.width, d.width), BF),
        slot_table=((d.slots, d.slot_devices), jnp.int32),
        cotangent=(cotangent.shape, BF),
        slab=((d.width, 256), BF),
        weight_t=((d.width, d.width), BF),
        proj=((d.width, 256), BF),
        matrix=((d.nrow * BLK, 4 * BLK), BF),
        out_a=((d.na, d.ny, 16, BLK), BF),
        out_b=((d.nb, 16, d.nz * BLK), BF),
        got_a=((d.ny, d.na * 16, BLK), BF),
        got_b=((d.nb * 16, d.nz * BLK), BF),
        spread_slots=((d.slots, d.na * 16), F32),
        to_row=((d.ny + 1, 1, d.na * 16), F32),
        joined=((d.ncol, 2, 8, 256), F32),
        pick_a=((d.ny, dense_rows, d.na * 16), BF),
        pick_b=((dense_rows, d.nb * 16), BF),
        dense_a=((d.ny, dense_rows, BLK), BF),
        dense_b=((d.nz, dense_rows, BLK), BF),
        ring_got_a=((4 * hops_a, dense_rows // 2, BLK), BF),
        ring_got_b=((4 * hops_b, dense_rows // 2, BLK), BF),
        stage_a=((4 * hops_a, dense_rows // 2, BLK), BF),
        stage_b=((4 * hops_b, dense_rows // 2, BLK), BF),
        all_a=((d.ny, dense_rows, BLK), BF),
        all_b=((d.nz, dense_rows, BLK), BF),
        wide_a=((d.ny * d.blocks, 8, BLK), F32),
        wide_b=((d.nz * d.blocks, 8, BLK), F32),
        back_a=((d.na, 16, d.ny * BLK), BF),
        back_b=((d.nb, d.nz * 16, BLK), BF),
        grads_a=((d.width, d.nrow * BLK), BF),
        grads_b=((d.width, d.nrow * BLK), BF),
        wide=((2, d.width, 4 * BLK), F32),
        grad_y=((d.width, 256), BF),
        grad_slab=((d.width, 256), BF),
        parts=((2, d.width, half), F32),
        to_twin=((d.width, half), BF),
        twin=((d.width, half), BF),
        summed=((d.width, half), BF),
        spread=((d.ncol_b, 16, half), BF),
        mine=((16, half), F32),
        rows_all=((d.nz, 16, half), F32),
        final=((16, half), BF),
        whole=((2, d.width, half), BF),
    )
    semaphores = dict(
        send=15, recv=15, load=4, send_ra=1, send_rb=1, recv_ra=4 * hops_a, recv_rb=4 * hops_b
    )
    semaphores.update(recv_ga=4 * hops_a, recv_gb=4 * hops_b)
    names = tuple(inputs) + tuple(outputs) + tuple(scratch) + tuple(semaphores)
    mixed, feat_grad, weight_raw = pl.pallas_call(
        functools.partial(whole_kernel, d, 1.0 / math.sqrt(node_total), names),
        out_shape=tuple(v[0] for v in outputs.values()),
        in_specs=[v[1] for v in inputs.values()],
        out_specs=tuple(v[1] for v in outputs.values()),
        scratch_shapes=[pltpu.VMEM(*v) for v in scratch.values()]
        + [dma((n,)) for n in semaphores.values()],
        compiler_params=pltpu.CompilerParams(
            collective_id=0, has_side_effects=True, vmem_limit_bytes=LIMIT
        ),
        name="layer",
    )(*(v[0] for v in inputs.values()))
    return pl.pallas_call(
        finish_kernel,
        out_shape=(
            sds(cotangent.shape, BF), sds(feats.shape, BF), sds((d.width, d.width), F32)
        ),
        in_specs=[vmem] * 3,
        out_specs=(vmem,) * 3,
        name="finish",
    )(mixed, feat_grad, weight_raw)


def solution(mesh):
    d = Dims(mesh.shape["row"], mesh.shape["col"])
    placed = (
        P("col", "row"),
        P(),
        P(("row", "col"), None, None),
        P(("row", "col"), None),
        P(("row", "col"), None),
        P(),
        P("col", "row"),
    )
    node_total = d.nrow * d.ncol * 2 * BLK
    return jax.shard_map(
        functools.partial(body, d, node_total),
        mesh=mesh,
        in_specs=placed,
        out_specs=(P("col", "row"), P("col", "row"), P()),
        check_vma=False,
    )
```

```python
import functools
import math
import types

import jax
import jax.numpy as jnp
from jax import lax
from jax.experimental import pallas as pl
from jax.experimental.pallas import tpu as pltpu
from jax.sharding import PartitionSpec as P

BF = jnp.bfloat16
F32 = jnp.float32
MESH = pl.DeviceIdType.MESH
NK = 2
CAP = 2
BLK = 128
LIMIT = 56 * 1024 * 1024


class Dims:
    def __init__(self, n_row, n_col):
        self.nrow, self.ncol = n_row, n_col
        self.nx = 4 if n_col > 4 else 2
        self.ny, self.nz = n_row // NK, n_col // self.nx
        self.width = 16 * n_col
        self.blocks = 2 * n_col
        self.slots = CAP * n_row
        self.na = NK * n_col
        self.nb = n_row * self.nx
        self.ncol_b = self.nb // NK
        self.slot_devices = n_row * n_col
        assert self.na == self.nb

    def here(self):
        r, c = lax.axis_index("row"), lax.axis_index("col")
        return r, c, r // NK, lax.rem(r, NK), c // self.nx, lax.rem(c, self.nx)


def remote(src, dst, send_sem, recv_sem, row, col):
    return pltpu.make_async_remote_copy(
        src_ref=src,
        dst_ref=dst,
        send_sem=send_sem,
        recv_sem=recv_sem,
        device_id=(row, col),
        device_id_type=MESH,
    )


def drain(ref, sem):
    pltpu.make_async_copy(ref, ref, sem).wait()


def each(start, stop, step):
    def run(i, carry):
        step(i)
        return carry

    lax.fori_loop(start, stop, run, 0)


def greet(barrier, row, col):
    pl.semaphore_signal(barrier, inc=1, device_id=(row, col), device_id_type=MESH)


def tile_of(inv, tiles, group, cap, source):
    at = inv[(group * CAP + cap) * 2 + source]
    value = tiles[jnp.maximum(at, 0)]
    return jnp.where(at >= 0, value, jnp.zeros_like(value))


def ways(n, way, piece):
    return n // 2 if way == piece else (n - 1) // 2


def offset_of(pos, n):
    if pos == 0:
        return n // 2
    return n // 2 - (pos + 1) // 2 if pos % 2 else -(n // 2 - pos // 2)


def pos_of(offset, n):
    if isinstance(offset, int):
        return [p for p in range(n) if (offset_of(p, n) - offset) % n == 0][0]
    return jnp.where(offset > n // 2, 2 * offset - n, jnp.maximum(n - 1 - 2 * offset, 0))


def parts_of(n):
    ends = (0, max(1, n - 3), n - 1, n)
    return [(a, b) for a, b in zip(ends, ends[1:]) if a < b]


class Ring:
    def __init__(self, n, me, rows, device, send, recv, recv_gather):
        self.n, self.me, self.half, self.device = n, me, rows // 2, device
        self.send, self.recv, self.recv_gather = send, recv, recv_gather
        self.hops = max(1, n // 2)

    def at(self, way, piece, step):
        return (way * 2 + piece) * self.hops + step

    def rows(self, piece):
        return pl.ds(piece * self.half, self.half)

    def near(self, offset):
        return lax.rem(self.me + offset + self.n, self.n)

    def copies(self):
        return sum(ways(self.n, w, p) for w in range(2) for p in range(2))

    def start(self, src, dst, way, piece, step, recv):
        row, col = self.device(self.near(1 - 2 * way))
        at = self.at(way, piece, step)
        remote(src, dst, self.send.at[0], recv.at[at], row, col).start()

    def reduce_step(self, step, dense, got, stage, part):
        for piece in range(2):
            for way in range(2):
                hops = ways(self.n, way, piece)
                if step >= hops:
                    continue
                to = pos_of((1 - 2 * way) * (hops - step), self.n)
                if not part[0] <= to < part[1]:
                    continue
                if step == 0:
                    src = dense.at[to, self.rows(piece)]
                else:
                    old = self.at(way, piece, step - 1)
                    drain(got.at[old], self.recv.at[old])
                    new = self.at(way, piece, step)
                    total = got[old].astype(F32) + dense[to, self.rows(piece)].astype(F32)
                    stage[new] = total.astype(BF)
                    src = stage.at[new]
                self.start(src, got.at[self.at(way, piece, step)], way, piece, step, self.recv)

    def reduce_end(self, piece, got):
        ends = []
        for way in range(2):
            hops = ways(self.n, way, piece)
            if hops:
                at = self.at(way, piece, hops - 1)
                drain(got.at[at], self.recv.at[at])
                ends.append(at)
        return ends

    def gather_step(self, step, piece, held, widen):
        for way in range(2):
            hops = ways(self.n, way, piece)
            if step > hops or hops == 0:
                continue
            src = self.near(-(1 - 2 * way) * step)
            pos = pos_of(-(1 - 2 * way) * step, self.n)
            part = held.at[src, self.rows(piece)]
            if step:
                drain(part, self.recv_gather.at[self.at(way, piece, step - 1)])
            if step < hops:
                self.start(part, part, way, piece, step, self.recv_gather)
            if step:
                widen(src, pos, piece)


def whole_kernel(d, scale, names, *refs):
    m = types.SimpleNamespace(**dict(zip(names, refs)))
    r, c, y, k, z, x = d.here()
    me_a, me_b = k * d.ncol + c, r * d.nx + x
    half = d.width // 2
    send, recv = m.send, m.recv
    barrier = pltpu.get_barrier_semaphore()

    def turn(i, n):
        j = (i + 1) // 2
        return jnp.where(lax.rem(i, 2) == 1, j, lax.rem(n - j, n))

    x_of = [lax.rem(x + j, d.nx) for j in range(d.nx)]
    k_of = [k, 1 - k]

    def line_a(other, jz, visit):
        first = isinstance(jz, int)
        to_z = z if first else lax.rem(z + turn(jz, d.nz), d.nz)
        for j in range(1 if first and not other else 0, d.nx):
            visit(y * NK + k_of[other], to_z * d.nx + x_of[j], k_of[other])

    def line_b(other, jy, visit):
        first = isinstance(jy, int)
        to_y = y if first else lax.rem(y + turn(jy, d.ny), d.ny)
        for j in range(1 if first and not other else 0, d.nx):
            visit(to_y * NK + k_of[other], z * d.nx + x_of[j], to_y, x_of[j])

    def peers_a(other, visit):
        line_a(other, 0, visit)
        each(1, d.nz, lambda jz: line_a(other, jz, visit))

    def peers_b(other, visit):
        line_b(other, 0, visit)
        each(1, d.ny, lambda jy: line_b(other, jy, visit))

    loads = [
        pltpu.make_async_copy(src, dst, m.load.at[at])
        for at, (src, dst) in enumerate(
            (
                (m.tiles_in, m.tiles),
                (m.weight_in, m.weight),
                (m.slot_table_in, m.slot_table),
                (m.cotangent_in, m.cotangent),
            )
        )
    ]
    for load in loads:
        load.start()
    for other in range(NK):
        peers_a(other, lambda row, col, _: greet(barrier, row, col))
        peers_b(other, lambda row, col, *_: greet(barrier, row, col))

    def place(group):
        offset = lax.rem(group // NK - y + d.ny, d.ny)
        at = pl.multiple_of((lax.rem(group, NK) * d.ny + pos_of(offset, d.ny)) * BLK, BLK)
        for cap in range(CAP):
            for s in range(2):
                lanes = slice((cap * 2 + s) * BLK, (cap * 2 + s + 1) * BLK)
                m.matrix[pl.ds(at, BLK), lanes] = tile_of(m.inv, m.tiles, group, cap, s)

    pl.semaphore_wait(barrier, d.na - 1 + d.nb - 1)

    def nodes_of(col):
        return m.feats.at[:, pl.ds(pl.multiple_of(col * 256, 256), 256)]

    own_rows = m.slab.at[pl.ds(pl.multiple_of(c * 16, 16), 16)]
    pltpu.make_async_copy(nodes_of(c), own_rows, recv.at[0]).start()

    def send_feats(row, col, _):
        remote(nodes_of(col), own_rows, send.at[0], recv.at[0], row, col).start()

    peers_a(0, send_feats)
    loads[0].wait()
    each(0, d.nrow, place)
    loads[1].wait()
    m.weight_t[...] = m.weight[...].T
    drain(m.slab, recv.at[0])
    value = jnp.dot(m.weight_t[...], m.slab[...], preferred_element_type=F32)
    value = value.reshape(d.ncol, 2, 8, 256)
    value = jnp.concatenate([value[:, 0], value[:, 1]], axis=0)
    m.proj[...] = value.reshape(d.width, 256).astype(BF)

    parts = parts_of(d.ny)
    last_part = len(parts) - 1
    spans = [pl.ds(a, b - a) for a, b in parts]
    lane_spans = [pl.ds(a * BLK, (b - a) * BLK) for a, b in parts]
    lanes_of = [
        pl.ds(pl.multiple_of(pos_of(lax.rem(j - z + d.nz, d.nz), d.nz) * BLK, BLK), BLK)
        for j in range(d.nz)
    ]

    def send_b(group, late):
        lanes, sem = lane_spans[late], 15 + late

        def send_to(to_x):
            src = m.out_b.at[group * d.nx + to_x, :, lanes]
            dst = m.got_b.at[pl.ds(pl.multiple_of(me_b * 16, 16), 16), lanes]
            remote(src, dst, send.at[sem], recv.at[sem], group, z * d.nx + to_x).start()

        @pl.when(group != r)
        def _():
            send_to(x)

        for j in range(1, d.nx):
            send_to(x_of[j])

    def group_step(gk, pos):
        gy = lax.rem(y + offset_of(pos, d.ny) + d.ny, d.ny)
        group = gy * NK + gk
        at = pl.multiple_of((gk * d.ny + pos) * BLK, BLK)
        both = jnp.concatenate(
            [m.matrix[pl.ds(at, BLK), : 2 * BLK], m.matrix[pl.ds(at, BLK), 2 * BLK :]], axis=0
        )
        part = lax.dot_general(
            m.proj[...], both, (((1,), (1,)), ((), ())), preferred_element_type=F32
        )
        first = part[:, :BLK].reshape(2 * d.ncol, 8, BLK)
        second = part[:, BLK:].reshape(2 * d.ncol, 8, BLK)
        packed = jnp.concatenate([first, second], axis=1).astype(BF)
        m.out_a[pl.ds(gk * d.ncol, d.ncol), pos] = packed[: d.ncol]
        for to_x in range(d.nx):
            for to_z in range(d.nz):
                m.out_b[group * d.nx + to_x, :, lanes_of[to_z]] = packed[
                    d.ncol + to_z * d.nx + to_x
                ]
        send_b(group, 0)

    def send_a(late):
        part, sem = spans[late], 12 + late
        dst = m.got_a.at[part, pl.ds(pl.multiple_of(me_a * 16, 16), 16)]

        def visit(row, col, to_k):
            src = m.out_a.at[to_k * d.ncol + col, part]
            remote(src, dst, send.at[sem], recv.at[sem], row, col).start()

        return visit

    for late in range(len(parts)):
        for first_k in range(2):
            for pos in range(*parts[late]):
                group_step(k_of[first_k], pos)
            if late == 0:
                peers_a(first_k, send_a(0))
    for late in range(len(parts)):
        if late:
            each(0, d.nrow, lambda i: send_b(lax.rem(r + i, d.nrow), late))
            for other in range(NK):
                peers_a(other, send_a(late))
        pltpu.make_async_copy(
            m.out_a.at[me_a, spans[late]],
            m.got_a.at[spans[late], pl.ds(pl.multiple_of(me_a * 16, 16), 16)],
            recv.at[12 + late],
        ).start()
        pltpu.make_async_copy(
            m.out_b.at[me_b, :, lane_spans[late]],
            m.got_b.at[pl.ds(pl.multiple_of(me_b * 16, 16), 16), lane_spans[late]],
            recv.at[15 + late],
        ).start()

    lane = lax.broadcasted_iota(jnp.int32, (d.slot_devices, d.na * 16), 1)
    device = lax.broadcasted_iota(jnp.int32, (d.slot_devices, d.na * 16), 0)
    src = lane // 16
    loads[2].wait()
    table = m.slot_table[...].astype(F32).astype(BF)
    row_lane = lax.broadcasted_iota(jnp.int32, (1, d.na * 16), 1)
    slot_id = lax.broadcasted_iota(jnp.int32, (d.slots, d.na * 16), 0)
    slot_lane = lax.broadcasted_iota(jnp.int32, (d.slots, d.na * 16), 1)
    lane_cap = lax.rem(slot_lane, 16) // 8
    feature = lax.rem(row_lane, 8).astype(F32)

    def targets(owner):
        onehot = jnp.where(device == owner, 1.0, 0.0).astype(BF)
        m.spread_slots[...] = lax.dot_general(
            table, onehot, (((1,), (0,)), ((), ())), preferred_element_type=F32
        )

    def target_row(group):
        wanted = slot_id == group * CAP + lane_cap
        block = jnp.sum(jnp.where(wanted, m.spread_slots[...], 0.0), axis=0, keepdims=True)
        return block * 8.0 + feature

    targets((src // d.nx) * d.ncol + z * d.nx + lax.rem(src, d.nx))
    m.to_row[d.ny] = target_row(r)
    targets(y * d.na + src)

    for pos in range(d.ny):
        gy = lax.rem(y + offset_of(pos, d.ny) + d.ny, d.ny)
        m.to_row[pos] = target_row(gy * NK + k)
    dense_rows = d.blocks * 8
    row_id = lax.broadcasted_iota(jnp.int32, (dense_rows, d.na * 16), 0).astype(F32)

    def selector(at):
        return jnp.where(row_id == m.to_row[at], 1.0, 0.0).astype(BF)

    m.pick_b[...] = selector(d.ny)

    def keep_pick(pos):
        m.pick_a[pos] = selector(pos)

    each(0, d.ny, keep_pick)
    ring_a = Ring(d.ny, y, dense_rows, lambda j: (j * NK + k, c), m.send_ra, m.recv_ra, m.recv_ga)
    ring_b = Ring(d.nz, z, dense_rows, lambda j: (r, j * d.nx + x), m.send_rb, m.recv_rb, m.recv_gb)

    def aggregate_a(pos):
        m.dense_a[pos] = jnp.dot(
            m.pick_a[pos], m.got_a[pos], preferred_element_type=F32
        ).astype(BF)

    def aggregate_b(first, stop):
        lanes = slice(first * BLK, stop * BLK)
        total = jnp.dot(m.pick_b[...], m.got_b[:, lanes], preferred_element_type=F32).astype(BF)
        for pos in range(first, stop):
            m.dense_b[pos] = total[:, (pos - first) * BLK : (pos - first + 1) * BLK]

    for late, part in enumerate(parts):
        drain(m.got_b.at[:, lane_spans[late]], recv.at[15 + late])
        aggregate_b(*part)
        drain(m.got_a.at[spans[late]], recv.at[12 + late])
        each(part[0], part[1], aggregate_a)
        for step in range(d.ny // 2):
            ring_b.reduce_step(step, m.dense_b, m.ring_got_b, m.stage_b, part)
            ring_a.reduce_step(step, m.dense_a, m.ring_got_a, m.stage_a, part)

    loads[3].wait()

    def widen_a(src, pos, piece):
        n = d.blocks // 2
        m.wide_a[pl.ds(pos * d.blocks + piece * n, n)] = (
            m.all_a[src, ring_a.rows(piece)].astype(F32).reshape(n, 8, BLK)
        )

    def widen_b(src, pos, piece):
        n = d.blocks // 2
        m.wide_b[pl.ds(pos * d.blocks + piece * n, n)] = (
            m.all_b[src, ring_b.rows(piece)].astype(F32).reshape(n, 8, BLK)
        )

    for piece in range(2):
        ends_b = ring_b.reduce_end(piece, m.ring_got_b)
        ends_a = ring_a.reduce_end(piece, m.ring_got_a)
        first = piece * d.blocks // 4

        def activate(p):
            rows = pl.ds(pl.multiple_of(p * 16, 16), 16)
            local = pl.ds(pl.multiple_of((p - first) * 16, 16), 16)
            sum_a = m.dense_a[d.ny - 1, rows].astype(F32)
            for at in ends_a:
                sum_a += m.ring_got_a[at, local].astype(F32)
            sum_b = m.dense_b[d.nz - 1, rows].astype(F32)
            for at in ends_b:
                sum_b += m.ring_got_b[at, local].astype(F32)
            low, high = [], []
            for part in range(2):
                pick = slice(part * 8, part * 8 + 8)
                pre = jnp.concatenate([sum_a[pick], sum_b[pick]], axis=0)
                lanes = pl.ds(pl.multiple_of((p * 2 + part) * BLK, BLK), BLK)
                sigma = jax.nn.sigmoid(pre)
                m.mixed[:, lanes] = (pre * sigma).astype(BF)
                grad = m.cotangent[:, lanes].astype(F32) * sigma * (1.0 + pre * (1.0 - sigma))
                low.append(grad[:8])
                high.append(grad[8:])
            m.all_a[y, rows] = jnp.concatenate(low, axis=0).astype(BF)
            m.all_b[z, rows] = jnp.concatenate(high, axis=0).astype(BF)

        each(first, first + d.blocks // 4, activate)
        ring_a.gather_step(0, piece, m.all_a, widen_a)
        ring_b.gather_step(0, piece, m.all_b, widen_b)
        widen_a(y, d.ny - 1, piece)
        widen_b(z, d.nz - 1, piece)

    def gathers(step):
        for piece in range(2):
            ring_a.gather_step(step, piece, m.all_a, widen_a)
            ring_b.gather_step(step, piece, m.all_b, widen_b)

    def columns(first, stop):
        return pl.ds(pl.multiple_of((k * d.ny + first) * BLK, BLK), (stop - first) * BLK)

    def column(to_y):
        pos = pos_of(lax.rem(y - to_y + d.ny, d.ny), d.ny)
        return pl.ds(pl.multiple_of((k * d.ny + pos) * BLK, BLK), BLK)

    group_slot = [
        (lax.rem(y + offset_of(pos, d.ny) + d.ny, d.ny) * NK + k) * CAP for pos in range(d.ny)
    ]

    def give_a(far, row, col, to_k):
        first, stop = parts[far]
        a, device = to_k * d.ncol + col, row * d.ncol + col
        for pos in range(first, stop):
            rows = [
                m.wide_a[pos * d.blocks + m.slots[group_slot[pos] + cap, device]]
                for cap in range(CAP)
            ]
            m.back_a[a, :, pos * BLK : (pos + 1) * BLK] = jnp.concatenate(rows, axis=0).astype(BF)
        src = m.back_a.at[a, :, pl.ds(first * BLK, (stop - first) * BLK)]
        return src, m.grads_a.at[pl.ds(pl.multiple_of(c * 16, 16), 16), columns(first, stop)]

    def give_b(far, row, col, to_y, to_x):
        first, stop = parts[far]
        b, device = row * d.nx + to_x, row * d.ncol + col
        at = [m.slots[r * CAP + cap, device] for cap in range(CAP)]
        for pos in range(first, stop):
            rows = [m.wide_b[pos * d.blocks + at[cap]] for cap in range(CAP)]
            m.back_b[b, pos * 16 : pos * 16 + 16] = jnp.concatenate(rows, axis=0).astype(BF)
        src = m.back_b.at[b, pl.ds(first * 16, (stop - first) * 16)]
        to_rows = pl.ds(pl.multiple_of((x * d.nz + first) * 16, 16), (stop - first) * 16)
        return src, m.grads_b.at[to_rows, column(to_y)]

    def give(far, other, start, stop):
        sem_a, sem_b = 18 + far, 21 + far

        def visit_a(row, col, to_k):
            src, dst = give_a(far, row, col, to_k)
            remote(src, dst, send.at[sem_a], recv.at[sem_a], row, col).start()

        def visit_b(row, col, to_y, to_x):
            src, dst = give_b(far, row, col, to_y, to_x)
            remote(src, dst, send.at[sem_b], recv.at[sem_b], row, col).start()

        def both_lines(j):
            line_a(other, j, visit_a)
            line_b(other, j, visit_b)

        if start == 0:
            both_lines(0)
        each(max(1, start), stop, both_lines)

    def keep(far):
        sem_a, sem_b = 18 + far, 21 + far
        src, dst = give_a(far, r, c, k)
        pltpu.make_async_copy(src, dst, recv.at[sem_a]).start()
        src, dst = give_b(far, r, c, y, x)
        pltpu.make_async_copy(src, dst, recv.at[sem_b]).start()

    top, mid = d.ny // 2, d.ny // 2
    own, far = last_part, 0
    give(own, 0, 0, d.ny)
    gathers(1)
    give(own, 1, 0, d.ny)
    if len(parts) > 2:
        give(1, 0, 0, mid)
        gathers(2)
        give(1, 0, mid, d.ny)
        gathers(3)
        give(1, 1, 0, mid)
        gathers(4)
        give(1, 1, mid, d.ny)
    give(far, 0, 0, d.ny)
    give(far, 1, 0, d.ny)
    for part in range(len(parts)):
        keep(part)

    span = d.ny * BLK
    near = parts[0][1]

    def multiply(first, stop, fresh):
        for half_k in range(NK):
            lanes = slice(half_k * span + first * BLK, half_k * span + stop * BLK)
            value = jnp.dot(m.grads_a[:, lanes], m.matrix[lanes, :], preferred_element_type=F32)
            m.wide[0] = value if fresh and half_k == 0 else m.wide[0] + value
        rows = jnp.concatenate(
            [
                m.grads_b[(j * d.nz + first) * 16 : (j * d.nz + stop) * 16]
                for j in range(d.nx)
            ],
            axis=0,
        )
        value = jnp.dot(rows, m.matrix[...], preferred_element_type=F32)
        count = (stop - first) * 16
        for j in range(d.nx):
            m.wide[1, (j * d.nz + first) * 16 : (j * d.nz + stop) * 16] = value[
                j * count : (j + 1) * count
            ]

    def arrived(part):
        count = parts[part][1] - parts[part][0]
        drain(m.grads_a.at[:, pl.ds(0, NK * count * BLK)], recv.at[18 + part])
        drain(m.grads_b.at[pl.ds(0, d.nx * count * 16)], recv.at[21 + part])

    for part in range(1, len(parts)):
        arrived(part)
    multiply(near, d.ny, True)
    arrived(0)
    multiply(0, near, False)

    def join(path):
        value = m.wide[path].reshape(d.ncol, CAP, 8, 4 * BLK)
        return value[:, 0, :, : 2 * BLK] + value[:, 1, :, 2 * BLK :]

    m.joined[:, 0] = join(0)
    high = join(1).reshape(d.nx, d.nz, 8, 256)
    for pos in range(d.nz):
        to_z = lax.rem(z + offset_of(pos, d.nz) + d.nz, d.nz)
        m.joined[pl.ds(to_z * d.nx, d.nx), 1] = high[:, pos]
    m.grad_y[...] = m.joined[...].reshape(d.width, 256).astype(BF)

    part = lax.dot_general(
        m.slab[...], m.grad_y[...], (((1,), (1,)), ((), ())), preferred_element_type=F32
    )
    m.parts[0] = part[:, :half]
    m.parts[1] = part[:, half:]
    m.to_twin[...] = m.parts[1 - k].astype(BF)
    twin_row = y * NK + (1 - k)
    swap = remote(m.to_twin, m.twin, send.at[6], recv.at[6], twin_row, c)
    swap.start()
    m.grad_slab[...] = jnp.dot(
        m.weight[...], m.grad_y[...], preferred_element_type=F32
    ).astype(BF)
    swap.wait()
    m.summed[...] = (m.parts[k] + m.twin[...].astype(F32)).astype(BF)

    def rows_of(ref, at):
        return ref.at[pl.ds(pl.multiple_of(at * 16, 16), 16)]

    me_w = y * d.nx + x
    own_nodes = m.feat_grad.at[:, pl.ds(pl.multiple_of(c * 256, 256), 256)]
    pltpu.make_async_copy(rows_of(m.summed, me_w), m.spread.at[me_w], recv.at[7]).start()
    pltpu.make_async_copy(rows_of(m.grad_slab, c), own_nodes, recv.at[8]).start()

    def scatter(row, col, to_y, to_x):
        src = rows_of(m.summed, to_y * d.nx + to_x)
        remote(src, m.spread.at[me_w], send.at[7], recv.at[7], row, col).start()

    def features(row, col, _):
        remote(rows_of(m.grad_slab, col), own_nodes, send.at[8], recv.at[8], row, col).start()

    peers_b(0, scatter)
    peers_a(0, features)
    drain(m.spread, recv.at[7])
    total = m.spread[0].astype(F32)
    for j in range(1, d.ncol_b):
        total += m.spread[j].astype(F32)
    m.mine[...] = total
    pltpu.make_async_copy(m.mine, m.rows_all.at[z], recv.at[9]).start()

    def along_z(i):
        to = lax.rem(z + i, d.nz)
        remote(m.mine, m.rows_all.at[z], send.at[9], recv.at[9], r, to * d.nx + x).start()

    each(1, d.nz, along_z)
    drain(m.rows_all, recv.at[9])
    total = m.rows_all[0]
    for j in range(1, d.nz):
        total += m.rows_all[j]
    m.final[...] = (total * scale).astype(BF)
    own_rows_w = m.whole.at[k, pl.ds(pl.multiple_of(me_w * 16, 16), 16)]
    pltpu.make_async_copy(m.final, own_rows_w, recv.at[10]).start()

    def publish(row, col, to_y, to_x):
        remote(m.final, own_rows_w, send.at[10], recv.at[10], row, col).start()

    peers_b(0, publish)
    drain(m.whole.at[k], recv.at[10])
    share = remote(m.whole.at[k], m.whole.at[k], send.at[11], recv.at[11], twin_row, c)
    share.start()
    share.wait()
    m.weight_raw[...] = m.whole[...]
    drain(m.slab.at[pl.ds(0, d.width - 16)], send.at[0])
    rest = pl.ds(0, d.na - 1)
    for part, (first, stop) in enumerate(parts):
        drain(m.out_a.at[rest, spans[part]], send.at[12 + part])
        drain(m.out_b.at[rest, :, lane_spans[part]], send.at[15 + part])
        drain(m.back_a.at[rest, :, lane_spans[part]], send.at[18 + part])
        drain(m.back_b.at[rest, pl.ds(first * 16, (stop - first) * 16)], send.at[21 + part])
    for ring, got, sem in ((ring_a, m.ring_got_a, m.send_ra), (ring_b, m.ring_got_b, m.send_rb)):
        for _ in range(2):
            drain(got.at[pl.ds(0, ring.copies())], sem.at[0])
    drain(m.spread.at[pl.ds(0, d.ncol_b - 1)], send.at[7])
    drain(m.grad_slab.at[pl.ds(0, d.width - 16)], send.at[8])
    drain(m.rows_all.at[pl.ds(0, d.nz - 1)], send.at[9])
    drain(m.whole.at[0, pl.ds(0, d.width - 16)], send.at[10])
    drain(m.grad_slab, recv.at[8])


def finish_kernel(mixed_in, feat_in, weight_in, mixed, feat_grad, weight_grad):
    half = weight_in.shape[2]
    mixed[...] = mixed_in[...]
    feat_grad[...] = feat_in[...]
    weight_grad[:, :half] = weight_in[0].astype(F32)
    weight_grad[:, half:] = weight_in[1].astype(F32)


def body(d, node_total, feats, weight, tile_vals, tile_src, tile_slot, slot_block, cotangent):
    vmem = pl.BlockSpec(memory_space=pltpu.VMEM)
    smem = pl.BlockSpec(memory_space=pltpu.SMEM)
    anywhere = pl.BlockSpec(memory_space=pl.ANY)
    sds = jax.ShapeDtypeStruct
    pair = tile_slot[0] * 2 + tile_src[0]
    pair_ids = jnp.arange(2 * d.slots, dtype=jnp.int32)
    tile_ids = jnp.arange(tile_vals.shape[0], dtype=jnp.int32)
    inv = jnp.max(jnp.where(pair[:, None] == pair_ids[None, :], tile_ids[:, None], -1), axis=0)
    inputs = dict(
        inv=(inv, smem),
        slots=(slot_block.T, smem),
        slot_table_in=(slot_block.T, anywhere),
        feats=(feats, anywhere),
        weight_in=(weight, anywhere),
        tiles_in=(tile_vals, anywhere),
        cotangent_in=(cotangent, anywhere),
    )
    outputs = dict(
        mixed=(sds(cotangent.shape, BF), vmem),
        feat_grad=(sds(feats.shape, BF), anywhere),
        weight_raw=(sds((2, d.width, d.width // 2), BF), vmem),
    )
    half, dense_rows, hops_a, hops_b = d.width // 2, d.blocks * 8, max(1, d.ny // 2), max(1, d.nz // 2)
    dma = pltpu.SemaphoreType.DMA
    scratch = dict(
        tiles=(tile_vals.shape, BF),
        weight=((d.width, d.width), BF),
        slot_table=((d.slots, d.slot_devices), jnp.int32),
        cotangent=(cotangent.shape, BF),
        slab=((d.width, 256), BF),
        weight_t=((d.width, d.width), BF),
        proj=((d.width, 256), BF),
        matrix=((d.nrow * BLK, 4 * BLK), BF),
        out_a=((d.na, d.ny, 16, BLK), BF),
        out_b=((d.nb, 16, d.nz * BLK), BF),
        got_a=((d.ny, d.na * 16, BLK), BF),
        got_b=((d.nb * 16, d.nz * BLK), BF),
        spread_slots=((d.slots, d.na * 16), F32),
        to_row=((d.ny + 1, 1, d.na * 16), F32),
        joined=((d.ncol, 2, 8, 256), F32),
        pick_a=((d.ny, dense_rows, d.na * 16), BF),
        pick_b=((dense_rows, d.nb * 16), BF),
        dense_a=((d.ny, dense_rows, BLK), BF),
        dense_b=((d.nz, dense_rows, BLK), BF),
        ring_got_a=((4 * hops_a, dense_rows // 2, BLK), BF),
        ring_got_b=((4 * hops_b, dense_rows // 2, BLK), BF),
        stage_a=((4 * hops_a, dense_rows // 2, BLK), BF),
        stage_b=((4 * hops_b, dense_rows // 2, BLK), BF),
        all_a=((d.ny, dense_rows, BLK), BF),
        all_b=((d.nz, dense_rows, BLK), BF),
        wide_a=((d.ny * d.blocks, 8, BLK), F32),
        wide_b=((d.nz * d.blocks, 8, BLK), F32),
        back_a=((d.na, 16, d.ny * BLK), BF),
        back_b=((d.nb, d.nz * 16, BLK), BF),
        grads_a=((d.width, d.nrow * BLK), BF),
        grads_b=((d.width, d.nrow * BLK), BF),
        wide=((2, d.width, 4 * BLK), F32),
        grad_y=((d.width, 256), BF),
        grad_slab=((d.width, 256), BF),
        parts=((2, d.width, half), F32),
        to_twin=((d.width, half), BF),
        twin=((d.width, half), BF),
        summed=((d.width, half), BF),
        spread=((d.ncol_b, 16, half), BF),
        mine=((16, half), F32),
        rows_all=((d.nz, 16, half), F32),
        final=((16, half), BF),
        whole=((2, d.width, half), BF),
    )
    semaphores = dict(
        send=24, recv=24, load=4, send_ra=1, send_rb=1, recv_ra=4 * hops_a, recv_rb=4 * hops_b
    )
    semaphores.update(recv_ga=4 * hops_a, recv_gb=4 * hops_b)
    names = tuple(inputs) + tuple(outputs) + tuple(scratch) + tuple(semaphores)
    mixed, feat_grad, weight_raw = pl.pallas_call(
        functools.partial(whole_kernel, d, 1.0 / math.sqrt(node_total), names),
        out_shape=tuple(v[0] for v in outputs.values()),
        in_specs=[v[1] for v in inputs.values()],
        out_specs=tuple(v[1] for v in outputs.values()),
        scratch_shapes=[pltpu.VMEM(*v) for v in scratch.values()]
        + [dma((n,)) for n in semaphores.values()],
        compiler_params=pltpu.CompilerParams(
            collective_id=0, has_side_effects=True, vmem_limit_bytes=LIMIT
        ),
        name="layer",
    )(*(v[0] for v in inputs.values()))
    return pl.pallas_call(
        finish_kernel,
        out_shape=(
            sds(cotangent.shape, BF), sds(feats.shape, BF), sds((d.width, d.width), F32)
        ),
        in_specs=[vmem] * 3,
        out_specs=(vmem,) * 3,
        name="finish",
    )(mixed, feat_grad, weight_raw)


def solution(mesh):
    d = Dims(mesh.shape["row"], mesh.shape["col"])
    placed = (
        P("col", "row"),
        P(),
        P(("row", "col"), None, None),
        P(("row", "col"), None),
        P(("row", "col"), None),
        P(),
        P("col", "row"),
    )
    node_total = d.nrow * d.ncol * 2 * BLK
    return jax.shard_map(
        functools.partial(body, d, node_total),
        mesh=mesh,
        in_specs=placed,
        out_specs=(P("col", "row"), P("col", "row"), P()),
        check_vma=False,
    )
```

```python
import functools
import math
import types

import jax
import jax.numpy as jnp
from jax import lax
from jax.experimental import pallas as pl
from jax.experimental.pallas import tpu as pltpu
from jax.sharding import PartitionSpec as P

BF = jnp.bfloat16
F32 = jnp.float32
MESH = pl.DeviceIdType.MESH
NK = 2
CAP = 2
BLK = 128
LIMIT = 56 * 1024 * 1024


class Dims:
    def __init__(self, n_row, n_col):
        self.nrow, self.ncol = n_row, n_col
        self.nx = 4 if n_col > 4 else 2
        self.ny, self.nz = n_row // NK, n_col // self.nx
        self.width = 16 * n_col
        self.blocks = 2 * n_col
        self.slots = CAP * n_row
        self.na = NK * n_col
        self.nb = n_row * self.nx
        self.ncol_b = self.nb // NK
        self.slot_devices = n_row * n_col
        assert self.na == self.nb

    def here(self):
        r, c = lax.axis_index("row"), lax.axis_index("col")
        return r, c, r // NK, lax.rem(r, NK), c // self.nx, lax.rem(c, self.nx)


def remote(src, dst, send_sem, recv_sem, row, col):
    return pltpu.make_async_remote_copy(
        src_ref=src,
        dst_ref=dst,
        send_sem=send_sem,
        recv_sem=recv_sem,
        device_id=(row, col),
        device_id_type=MESH,
    )


def drain(ref, sem):
    pltpu.make_async_copy(ref, ref, sem).wait()


def each(start, stop, step, unroll=1):
    def run(i, carry):
        step(i)
        return carry

    lax.fori_loop(start, stop, run, 0, unroll=unroll)


def greet(barrier, row, col):
    pl.semaphore_signal(barrier, inc=1, device_id=(row, col), device_id_type=MESH)


def tile_of(inv, tiles, group, cap, source):
    at = inv[(group * CAP + cap) * 2 + source]
    value = tiles[jnp.maximum(at, 0)]
    return jnp.where(at >= 0, value, jnp.zeros_like(value))


def ways(n, way, piece):
    return n // 2 if way == piece else (n - 1) // 2


def offset_of(pos, n):
    if pos == 0:
        return n // 2
    return n // 2 - (pos + 1) // 2 if pos % 2 else -(n // 2 - pos // 2)


def pos_of(offset, n):
    if isinstance(offset, int):
        return [p for p in range(n) if (offset_of(p, n) - offset) % n == 0][0]
    return jnp.where(offset > n // 2, 2 * offset - n, jnp.maximum(n - 1 - 2 * offset, 0))


def parts_of(n):
    ends = (0, max(1, n - 3), n - 1, n)
    return [(a, b) for a, b in zip(ends, ends[1:]) if a < b]


class Ring:
    def __init__(self, n, me, rows, device, send, recv, recv_gather):
        self.n, self.me, self.half, self.device = n, me, rows // 2, device
        self.send, self.recv, self.recv_gather = send, recv, recv_gather
        self.hops = max(1, n // 2)

    def at(self, way, piece, step):
        return (way * 2 + piece) * self.hops + step

    def rows(self, piece):
        return pl.ds(piece * self.half, self.half)

    def near(self, offset):
        return lax.rem(self.me + offset + self.n, self.n)

    def copies(self):
        return sum(ways(self.n, w, p) for w in range(2) for p in range(2))

    def start(self, src, dst, way, piece, step, recv):
        row, col = self.device(self.near(1 - 2 * way))
        at = self.at(way, piece, step)
        remote(src, dst, self.send.at[0], recv.at[at], row, col).start()

    def reduce_step(self, step, dense, got, stage, part):
        for piece in range(2):
            for way in range(2):
                hops = ways(self.n, way, piece)
                if step >= hops:
                    continue
                to = pos_of((1 - 2 * way) * (hops - step), self.n)
                if not part[0] <= to < part[1]:
                    continue
                if step == 0:
                    src = dense.at[to, self.rows(piece)]
                else:
                    old = self.at(way, piece, step - 1)
                    drain(got.at[old], self.recv.at[old])
                    new = self.at(way, piece, step)
                    total = got[old].astype(F32) + dense[to, self.rows(piece)].astype(F32)
                    stage[new] = total.astype(BF)
                    src = stage.at[new]
                self.start(src, got.at[self.at(way, piece, step)], way, piece, step, self.recv)

    def reduce_end(self, piece, got):
        ends = []
        for way in range(2):
            hops = ways(self.n, way, piece)
            if hops:
                at = self.at(way, piece, hops - 1)
                drain(got.at[at], self.recv.at[at])
                ends.append(at)
        return ends

    def gather_step(self, step, piece, held, widen):
        for way in range(2):
            hops = ways(self.n, way, piece)
            if step > hops or hops == 0:
                continue
            src = self.near(-(1 - 2 * way) * step)
            pos = pos_of(-(1 - 2 * way) * step, self.n)
            part = held.at[src, self.rows(piece)]
            if step:
                drain(part, self.recv_gather.at[self.at(way, piece, step - 1)])
            if step < hops:
                self.start(part, part, way, piece, step, self.recv_gather)
            if step:
                widen(src, pos, piece)


def whole_kernel(d, scale, names, *refs):
    m = types.SimpleNamespace(**dict(zip(names, refs)))
    r, c, y, k, z, x = d.here()
    me_a, me_b = k * d.ncol + c, r * d.nx + x
    half = d.width // 2
    send, recv = m.send, m.recv
    barrier = pltpu.get_barrier_semaphore()

    def turn(i, n):
        j = (i + 1) // 2
        return jnp.where(lax.rem(i, 2) == 1, j, lax.rem(n - j, n))

    x_of = [lax.rem(x + j, d.nx) for j in range(d.nx)]
    k_of = [k, 1 - k]

    def line_a(other, jz, visit):
        first = isinstance(jz, int)
        to_z = z if first else lax.rem(z + turn(jz, d.nz), d.nz)
        for j in range(1 if first and not other else 0, d.nx):
            visit(y * NK + k_of[other], to_z * d.nx + x_of[j], k_of[other])

    def line_b(other, jy, visit):
        first = isinstance(jy, int)
        to_y = y if first else lax.rem(y + turn(jy, d.ny), d.ny)
        for j in range(1 if first and not other else 0, d.nx):
            visit(to_y * NK + k_of[other], z * d.nx + x_of[j], to_y, x_of[j])

    def peers_a(other, visit):
        line_a(other, 0, visit)
        each(1, d.nz, lambda jz: line_a(other, jz, visit))

    def peers_b(other, visit):
        line_b(other, 0, visit)
        each(1, d.ny, lambda jy: line_b(other, jy, visit))

    loads = [
        pltpu.make_async_copy(src, dst, m.load.at[at])
        for at, (src, dst) in enumerate(
            (
                (m.tiles_in, m.tiles),
                (m.weight_in, m.weight),
                (m.slot_table_in, m.slot_table),
                (m.cotangent_in, m.cotangent),
            )
        )
    ]
    for load in loads:
        load.start()
    for other in range(NK):
        peers_a(other, lambda row, col, _: greet(barrier, row, col))
        peers_b(other, lambda row, col, *_: greet(barrier, row, col))

    def place(group):
        offset = lax.rem(group // NK - y + d.ny, d.ny)
        at = pl.multiple_of((lax.rem(group, NK) * d.ny + pos_of(offset, d.ny)) * BLK, BLK)
        for cap in range(CAP):
            for s in range(2):
                lanes = slice((cap * 2 + s) * BLK, (cap * 2 + s + 1) * BLK)
                m.matrix[pl.ds(at, BLK), lanes] = tile_of(m.inv, m.tiles, group, cap, s)

    pl.semaphore_wait(barrier, d.na - 1 + d.nb - 1)

    def nodes_of(col):
        return m.feats.at[:, pl.ds(pl.multiple_of(col * 256, 256), 256)]

    own_rows = m.slab.at[pl.ds(pl.multiple_of(c * 16, 16), 16)]
    pltpu.make_async_copy(nodes_of(c), own_rows, recv.at[0]).start()

    def send_feats(row, col, _):
        remote(nodes_of(col), own_rows, send.at[0], recv.at[0], row, col).start()

    peers_a(0, send_feats)
    loads[0].wait()
    each(0, d.nrow, place)
    loads[1].wait()
    m.weight_t[...] = m.weight[...].T
    drain(m.slab, recv.at[0])
    value = jnp.dot(m.weight_t[...], m.slab[...], preferred_element_type=F32)
    value = value.reshape(d.ncol, 2, 8, 256)
    value = jnp.concatenate([value[:, 0], value[:, 1]], axis=0)
    m.proj[...] = value.reshape(d.width, 256).astype(BF)

    parts = parts_of(d.ny)
    last_part = len(parts) - 1
    spans = [pl.ds(a, b - a) for a, b in parts]
    lane_spans = [pl.ds(a * BLK, (b - a) * BLK) for a, b in parts]
    lanes_of = [
        pl.ds(pl.multiple_of(pos_of(lax.rem(j - z + d.nz, d.nz), d.nz) * BLK, BLK), BLK)
        for j in range(d.nz)
    ]

    def send_b(group, late):
        lanes, sem = lane_spans[late], 15 + late

        def send_to(to_x):
            src = m.out_b.at[group * d.nx + to_x, :, lanes]
            dst = m.got_b.at[pl.ds(pl.multiple_of(me_b * 16, 16), 16), lanes]
            remote(src, dst, send.at[sem], recv.at[sem], group, z * d.nx + to_x).start()

        @pl.when(group != r)
        def _():
            send_to(x)

        for j in range(1, d.nx):
            send_to(x_of[j])

    def group_step(gk, pos):
        gy = lax.rem(y + offset_of(pos, d.ny) + d.ny, d.ny)
        group = gy * NK + gk
        at = pl.multiple_of((gk * d.ny + pos) * BLK, BLK)
        both = jnp.concatenate(
            [m.matrix[pl.ds(at, BLK), : 2 * BLK], m.matrix[pl.ds(at, BLK), 2 * BLK :]], axis=0
        )
        part = lax.dot_general(
            m.proj[...], both, (((1,), (1,)), ((), ())), preferred_element_type=F32
        )
        first = part[:, :BLK].reshape(2 * d.ncol, 8, BLK)
        second = part[:, BLK:].reshape(2 * d.ncol, 8, BLK)
        packed = jnp.concatenate([first, second], axis=1).astype(BF)
        m.out_a[pl.ds(gk * d.ncol, d.ncol), pos] = packed[: d.ncol]
        for to_x in range(d.nx):
            for to_z in range(d.nz):
                m.out_b[group * d.nx + to_x, :, lanes_of[to_z]] = packed[
                    d.ncol + to_z * d.nx + to_x
                ]
        send_b(group, 0)

    def send_a(late):
        part, sem = spans[late], 12 + late
        dst = m.got_a.at[part, pl.ds(pl.multiple_of(me_a * 16, 16), 16)]

        def visit(row, col, to_k):
            src = m.out_a.at[to_k * d.ncol + col, part]
            remote(src, dst, send.at[sem], recv.at[sem], row, col).start()

        return visit

    for late in range(len(parts)):
        for first_k in range(2):
            for pos in range(*parts[late]):
                group_step(k_of[first_k], pos)
            if late == 0:
                peers_a(first_k, send_a(0))

    def bulk(late, other):
        first = other * d.nrow // NK
        each(first, first + d.nrow // NK, lambda i: send_b(lax.rem(r + i, d.nrow), late))
        peers_a(other, send_a(late))

    pending = [(late, other) for late in range(1, len(parts)) for other in range(NK)]
    bulk(*pending.pop(0))
    for late in range(len(parts)):
        pltpu.make_async_copy(
            m.out_a.at[me_a, spans[late]],
            m.got_a.at[spans[late], pl.ds(pl.multiple_of(me_a * 16, 16), 16)],
            recv.at[12 + late],
        ).start()
        pltpu.make_async_copy(
            m.out_b.at[me_b, :, lane_spans[late]],
            m.got_b.at[pl.ds(pl.multiple_of(me_b * 16, 16), 16), lane_spans[late]],
            recv.at[15 + late],
        ).start()

    lane = lax.broadcasted_iota(jnp.int32, (d.slot_devices, d.na * 16), 1)
    device = lax.broadcasted_iota(jnp.int32, (d.slot_devices, d.na * 16), 0)
    src = lane // 16
    loads[2].wait()
    table = m.slot_table[...].astype(F32).astype(BF)
    row_lane = lax.broadcasted_iota(jnp.int32, (1, d.na * 16), 1)
    slot_id = lax.broadcasted_iota(jnp.int32, (d.slots, d.na * 16), 0)
    slot_lane = lax.broadcasted_iota(jnp.int32, (d.slots, d.na * 16), 1)
    lane_cap = lax.rem(slot_lane, 16) // 8
    feature = lax.rem(row_lane, 8).astype(F32)

    def targets(owner):
        onehot = jnp.where(device == owner, 1.0, 0.0).astype(BF)
        m.spread_slots[...] = lax.dot_general(
            table, onehot, (((1,), (0,)), ((), ())), preferred_element_type=F32
        )

    def target_row(group):
        wanted = slot_id == group * CAP + lane_cap
        block = jnp.sum(jnp.where(wanted, m.spread_slots[...], 0.0), axis=0, keepdims=True)
        return block * 8.0 + feature

    targets((src // d.nx) * d.ncol + z * d.nx + lax.rem(src, d.nx))
    m.to_row[d.ny] = target_row(r)
    targets(y * d.na + src)

    for pos in range(d.ny):
        gy = lax.rem(y + offset_of(pos, d.ny) + d.ny, d.ny)
        m.to_row[pos] = target_row(gy * NK + k)
    dense_rows = d.blocks * 8
    row_id = lax.broadcasted_iota(jnp.int32, (dense_rows, d.na * 16), 0).astype(F32)

    def selector(at):
        return jnp.where(row_id == m.to_row[at], 1.0, 0.0).astype(BF)

    m.pick_b[...] = selector(d.ny)

    def keep_pick(pos):
        m.pick_a[pos] = selector(pos)

    each(0, d.ny, keep_pick)
    ring_a = Ring(d.ny, y, dense_rows, lambda j: (j * NK + k, c), m.send_ra, m.recv_ra, m.recv_ga)
    ring_b = Ring(d.nz, z, dense_rows, lambda j: (r, j * d.nx + x), m.send_rb, m.recv_rb, m.recv_gb)

    def aggregate_a(pos):
        m.dense_a[pos] = jnp.dot(
            m.pick_a[pos], m.got_a[pos], preferred_element_type=F32
        ).astype(BF)

    def aggregate_b(first, stop):
        lanes = slice(first * BLK, stop * BLK)
        total = jnp.dot(m.pick_b[...], m.got_b[:, lanes], preferred_element_type=F32).astype(BF)
        for pos in range(first, stop):
            m.dense_b[pos] = total[:, (pos - first) * BLK : (pos - first + 1) * BLK]

    for late, part in enumerate(parts):
        drain(m.got_b.at[:, lane_spans[late]], recv.at[15 + late])
        aggregate_b(*part)
        drain(m.got_a.at[spans[late]], recv.at[12 + late])
        each(part[0], part[1], aggregate_a)
        for step in range(d.ny // 2):
            ring_b.reduce_step(step, m.dense_b, m.ring_got_b, m.stage_b, part)
            ring_a.reduce_step(step, m.dense_a, m.ring_got_a, m.stage_a, part)
            if pending:
                bulk(*pending.pop(0))
        while pending:
            bulk(*pending.pop(0))

    loads[3].wait()

    def widen_a(src, pos, piece):
        n = d.blocks // 2
        m.wide_a[pl.ds(pos * d.blocks + piece * n, n)] = (
            m.all_a[src, ring_a.rows(piece)].astype(F32).reshape(n, 8, BLK)
        )

    def widen_b(src, pos, piece):
        n = d.blocks // 2
        m.wide_b[pl.ds(pos * d.blocks + piece * n, n)] = (
            m.all_b[src, ring_b.rows(piece)].astype(F32).reshape(n, 8, BLK)
        )

    for piece in range(2):
        ends_b = ring_b.reduce_end(piece, m.ring_got_b)
        ends_a = ring_a.reduce_end(piece, m.ring_got_a)
        first = piece * d.blocks // 4

        def activate(p):
            rows = pl.ds(pl.multiple_of(p * 16, 16), 16)
            local = pl.ds(pl.multiple_of((p - first) * 16, 16), 16)
            sum_a = m.dense_a[d.ny - 1, rows].astype(F32)
            for at in ends_a:
                sum_a += m.ring_got_a[at, local].astype(F32)
            sum_b = m.dense_b[d.nz - 1, rows].astype(F32)
            for at in ends_b:
                sum_b += m.ring_got_b[at, local].astype(F32)
            low, high = [], []
            for part in range(2):
                pick = slice(part * 8, part * 8 + 8)
                pre = jnp.concatenate([sum_a[pick], sum_b[pick]], axis=0)
                lanes = pl.ds(pl.multiple_of((p * 2 + part) * BLK, BLK), BLK)
                sigma = jax.nn.sigmoid(pre)
                m.mixed[:, lanes] = (pre * sigma).astype(BF)
                grad = m.cotangent[:, lanes].astype(F32) * sigma * (1.0 + pre * (1.0 - sigma))
                low.append(grad[:8])
                high.append(grad[8:])
            m.all_a[y, rows] = jnp.concatenate(low, axis=0).astype(BF)
            m.all_b[z, rows] = jnp.concatenate(high, axis=0).astype(BF)

        each(first, first + d.blocks // 4, activate, 2)
        ring_a.gather_step(0, piece, m.all_a, widen_a)
        ring_b.gather_step(0, piece, m.all_b, widen_b)
        widen_a(y, d.ny - 1, piece)
        widen_b(z, d.nz - 1, piece)

    def gathers(step):
        for piece in range(2):
            ring_a.gather_step(step, piece, m.all_a, widen_a)
            ring_b.gather_step(step, piece, m.all_b, widen_b)

    def columns(first, stop):
        return pl.ds(pl.multiple_of((k * d.ny + first) * BLK, BLK), (stop - first) * BLK)

    def column(to_y):
        pos = pos_of(lax.rem(y - to_y + d.ny, d.ny), d.ny)
        return pl.ds(pl.multiple_of((k * d.ny + pos) * BLK, BLK), BLK)

    group_slot = [
        (lax.rem(y + offset_of(pos, d.ny) + d.ny, d.ny) * NK + k) * CAP for pos in range(d.ny)
    ]

    def give_a(far, row, col, to_k):
        first, stop = parts[far]
        a, device = to_k * d.ncol + col, row * d.ncol + col
        for pos in range(first, stop):
            rows = [
                m.wide_a[pos * d.blocks + m.slots[group_slot[pos] + cap, device]]
                for cap in range(CAP)
            ]
            m.back_a[a, :, pos * BLK : (pos + 1) * BLK] = jnp.concatenate(rows, axis=0).astype(BF)
        src = m.back_a.at[a, :, pl.ds(first * BLK, (stop - first) * BLK)]
        return src, m.grads_a.at[pl.ds(pl.multiple_of(c * 16, 16), 16), columns(first, stop)]

    def give_b(far, row, col, to_y, to_x):
        first, stop = parts[far]
        b, device = row * d.nx + to_x, row * d.ncol + col
        at = [m.slots[r * CAP + cap, device] for cap in range(CAP)]
        for pos in range(first, stop):
            rows = [m.wide_b[pos * d.blocks + at[cap]] for cap in range(CAP)]
            m.back_b[b, pos * 16 : pos * 16 + 16] = jnp.concatenate(rows, axis=0).astype(BF)
        src = m.back_b.at[b, pl.ds(first * 16, (stop - first) * 16)]
        to_rows = pl.ds(pl.multiple_of((x * d.nz + first) * 16, 16), (stop - first) * 16)
        return src, m.grads_b.at[to_rows, column(to_y)]

    def give(far, other, start, stop):
        sem_a, sem_b = 18 + far, 21 + far

        def visit_a(row, col, to_k):
            src, dst = give_a(far, row, col, to_k)
            remote(src, dst, send.at[sem_a], recv.at[sem_a], row, col).start()

        def visit_b(row, col, to_y, to_x):
            src, dst = give_b(far, row, col, to_y, to_x)
            remote(src, dst, send.at[sem_b], recv.at[sem_b], row, col).start()

        def both_lines(j):
            line_a(other, j, visit_a)
            line_b(other, j, visit_b)

        if start == 0:
            both_lines(0)
        each(max(1, start), stop, both_lines)

    def keep(far):
        sem_a, sem_b = 18 + far, 21 + far
        src, dst = give_a(far, r, c, k)
        pltpu.make_async_copy(src, dst, recv.at[sem_a]).start()
        src, dst = give_b(far, r, c, y, x)
        pltpu.make_async_copy(src, dst, recv.at[sem_b]).start()

    top, mid = d.ny // 2, d.ny // 2
    own, far = last_part, 0
    give(own, 0, 0, d.ny)
    gathers(1)
    give(own, 1, 0, d.ny)
    if len(parts) > 2:
        give(1, 0, 0, mid)
        gathers(2)
        give(1, 0, mid, d.ny)
        gathers(3)
        give(1, 1, 0, mid)
        gathers(4)
        give(1, 1, mid, d.ny)
    give(far, 0, 0, d.ny)
    give(far, 1, 0, d.ny)
    for part in range(len(parts)):
        keep(part)

    span = d.ny * BLK
    near = parts[0][1]

    def multiply(first, stop, fresh):
        for half_k in range(NK):
            lanes = slice(half_k * span + first * BLK, half_k * span + stop * BLK)
            value = jnp.dot(m.grads_a[:, lanes], m.matrix[lanes, :], preferred_element_type=F32)
            m.wide[0] = value if fresh and half_k == 0 else m.wide[0] + value
        rows = jnp.concatenate(
            [
                m.grads_b[(j * d.nz + first) * 16 : (j * d.nz + stop) * 16]
                for j in range(d.nx)
            ],
            axis=0,
        )
        value = jnp.dot(rows, m.matrix[...], preferred_element_type=F32)
        count = (stop - first) * 16
        for j in range(d.nx):
            m.wide[1, (j * d.nz + first) * 16 : (j * d.nz + stop) * 16] = value[
                j * count : (j + 1) * count
            ]

    def arrived(part):
        count = parts[part][1] - parts[part][0]
        drain(m.grads_a.at[:, pl.ds(0, NK * count * BLK)], recv.at[18 + part])
        drain(m.grads_b.at[pl.ds(0, d.nx * count * 16)], recv.at[21 + part])

    for part in range(1, len(parts)):
        arrived(part)
    multiply(near, d.ny, True)
    arrived(0)
    multiply(0, near, False)

    def join(path):
        value = m.wide[path].reshape(d.ncol, CAP, 8, 4 * BLK)
        return value[:, 0, :, : 2 * BLK] + value[:, 1, :, 2 * BLK :]

    m.joined[:, 0] = join(0)
    high = join(1).reshape(d.nx, d.nz, 8, 256)
    for pos in range(d.nz):
        to_z = lax.rem(z + offset_of(pos, d.nz) + d.nz, d.nz)
        m.joined[pl.ds(to_z * d.nx, d.nx), 1] = high[:, pos]
    m.grad_y[...] = m.joined[...].reshape(d.width, 256).astype(BF)

    part = lax.dot_general(
        m.slab[...], m.grad_y[...], (((1,), (1,)), ((), ())), preferred_element_type=F32
    )
    m.parts[0] = part[:, :half]
    m.parts[1] = part[:, half:]
    m.to_twin[...] = m.parts[1 - k].astype(BF)
    twin_row = y * NK + (1 - k)
    swap = remote(m.to_twin, m.twin, send.at[6], recv.at[6], twin_row, c)
    swap.start()
    m.grad_slab[...] = jnp.dot(
        m.weight[...], m.grad_y[...], preferred_element_type=F32
    ).astype(BF)
    swap.wait()
    m.summed[...] = (m.parts[k] + m.twin[...].astype(F32)).astype(BF)

    def rows_of(ref, at):
        return ref.at[pl.ds(pl.multiple_of(at * 16, 16), 16)]

    me_w = y * d.nx + x
    own_nodes = m.feat_grad.at[:, pl.ds(pl.multiple_of(c * 256, 256), 256)]
    pltpu.make_async_copy(rows_of(m.summed, me_w), m.spread.at[me_w], recv.at[7]).start()
    pltpu.make_async_copy(rows_of(m.grad_slab, c), own_nodes, recv.at[8]).start()

    def scatter(row, col, to_y, to_x):
        src = rows_of(m.summed, to_y * d.nx + to_x)
        remote(src, m.spread.at[me_w], send.at[7], recv.at[7], row, col).start()

    def features(row, col, _):
        remote(rows_of(m.grad_slab, col), own_nodes, send.at[8], recv.at[8], row, col).start()

    peers_b(0, scatter)
    peers_a(0, features)
    drain(m.spread, recv.at[7])
    total = m.spread[0].astype(F32)
    for j in range(1, d.ncol_b):
        total += m.spread[j].astype(F32)
    m.mine[...] = total
    pltpu.make_async_copy(m.mine, m.rows_all.at[z], recv.at[9]).start()

    def along_z(i):
        to = lax.rem(z + i, d.nz)
        remote(m.mine, m.rows_all.at[z], send.at[9], recv.at[9], r, to * d.nx + x).start()

    each(1, d.nz, along_z)
    drain(m.rows_all, recv.at[9])
    total = m.rows_all[0]
    for j in range(1, d.nz):
        total += m.rows_all[j]
    m.final[...] = (total * scale).astype(BF)
    own_rows_w = m.whole.at[k, pl.ds(pl.multiple_of(me_w * 16, 16), 16)]
    pltpu.make_async_copy(m.final, own_rows_w, recv.at[10]).start()

    def publish(row, col, to_y, to_x):
        remote(m.final, own_rows_w, send.at[10], recv.at[10], row, col).start()

    peers_b(0, publish)
    drain(m.whole.at[k], recv.at[10])
    share = remote(m.whole.at[k], m.whole.at[k], send.at[11], recv.at[11], twin_row, c)
    share.start()
    share.wait()
    m.weight_raw[...] = m.whole[...]
    drain(m.slab.at[pl.ds(0, d.width - 16)], send.at[0])
    rest = pl.ds(0, d.na - 1)
    for part, (first, stop) in enumerate(parts):
        drain(m.out_a.at[rest, spans[part]], send.at[12 + part])
        drain(m.out_b.at[rest, :, lane_spans[part]], send.at[15 + part])
        drain(m.back_a.at[rest, :, lane_spans[part]], send.at[18 + part])
        drain(m.back_b.at[rest, pl.ds(first * 16, (stop - first) * 16)], send.at[21 + part])
    for ring, got, sem in ((ring_a, m.ring_got_a, m.send_ra), (ring_b, m.ring_got_b, m.send_rb)):
        for _ in range(2):
            drain(got.at[pl.ds(0, ring.copies())], sem.at[0])
    drain(m.spread.at[pl.ds(0, d.ncol_b - 1)], send.at[7])
    drain(m.grad_slab.at[pl.ds(0, d.width - 16)], send.at[8])
    drain(m.rows_all.at[pl.ds(0, d.nz - 1)], send.at[9])
    drain(m.whole.at[0, pl.ds(0, d.width - 16)], send.at[10])
    drain(m.grad_slab, recv.at[8])


def finish_kernel(mixed_in, feat_in, weight_in, mixed, feat_grad, weight_grad):
    half = weight_in.shape[2]
    mixed[...] = mixed_in[...]
    feat_grad[...] = feat_in[...]
    weight_grad[:, :half] = weight_in[0].astype(F32)
    weight_grad[:, half:] = weight_in[1].astype(F32)


def body(d, node_total, feats, weight, tile_vals, tile_src, tile_slot, slot_block, cotangent):
    vmem = pl.BlockSpec(memory_space=pltpu.VMEM)
    smem = pl.BlockSpec(memory_space=pltpu.SMEM)
    anywhere = pl.BlockSpec(memory_space=pl.ANY)
    sds = jax.ShapeDtypeStruct
    pair = tile_slot[0] * 2 + tile_src[0]
    pair_ids = jnp.arange(2 * d.slots, dtype=jnp.int32)
    tile_ids = jnp.arange(tile_vals.shape[0], dtype=jnp.int32)
    inv = jnp.max(jnp.where(pair[:, None] == pair_ids[None, :], tile_ids[:, None], -1), axis=0)
    inputs = dict(
        inv=(inv, smem),
        slots=(slot_block.T, smem),
        slot_table_in=(slot_block.T, anywhere),
        feats=(feats, anywhere),
        weight_in=(weight, anywhere),
        tiles_in=(tile_vals, anywhere),
        cotangent_in=(cotangent, anywhere),
    )
    outputs = dict(
        mixed=(sds(cotangent.shape, BF), vmem),
        feat_grad=(sds(feats.shape, BF), anywhere),
        weight_raw=(sds((2, d.width, d.width // 2), BF), vmem),
    )
    half, dense_rows, hops_a, hops_b = d.width // 2, d.blocks * 8, max(1, d.ny // 2), max(1, d.nz // 2)
    dma = pltpu.SemaphoreType.DMA
    scratch = dict(
        tiles=(tile_vals.shape, BF),
        weight=((d.width, d.width), BF),
        slot_table=((d.slots, d.slot_devices), jnp.int32),
        cotangent=(cotangent.shape, BF),
        slab=((d.width, 256), BF),
        weight_t=((d.width, d.width), BF),
        proj=((d.width, 256), BF),
        matrix=((d.nrow * BLK, 4 * BLK), BF),
        out_a=((d.na, d.ny, 16, BLK), BF),
        out_b=((d.nb, 16, d.nz * BLK), BF),
        got_a=((d.ny, d.na * 16, BLK), BF),
        got_b=((d.nb * 16, d.nz * BLK), BF),
        spread_slots=((d.slots, d.na * 16), F32),
        to_row=((d.ny + 1, 1, d.na * 16), F32),
        joined=((d.ncol, 2, 8, 256), F32),
        pick_a=((d.ny, dense_rows, d.na * 16), BF),
        pick_b=((dense_rows, d.nb * 16), BF),
        dense_a=((d.ny, dense_rows, BLK), BF),
        dense_b=((d.nz, dense_rows, BLK), BF),
        ring_got_a=((4 * hops_a, dense_rows // 2, BLK), BF),
        ring_got_b=((4 * hops_b, dense_rows // 2, BLK), BF),
        stage_a=((4 * hops_a, dense_rows // 2, BLK), BF),
        stage_b=((4 * hops_b, dense_rows // 2, BLK), BF),
        all_a=((d.ny, dense_rows, BLK), BF),
        all_b=((d.nz, dense_rows, BLK), BF),
        wide_a=((d.ny * d.blocks, 8, BLK), F32),
        wide_b=((d.nz * d.blocks, 8, BLK), F32),
        back_a=((d.na, 16, d.ny * BLK), BF),
        back_b=((d.nb, d.nz * 16, BLK), BF),
        grads_a=((d.width, d.nrow * BLK), BF),
        grads_b=((d.width, d.nrow * BLK), BF),
        wide=((2, d.width, 4 * BLK), F32),
        grad_y=((d.width, 256), BF),
        grad_slab=((d.width, 256), BF),
        parts=((2, d.width, half), F32),
        to_twin=((d.width, half), BF),
        twin=((d.width, half), BF),
        summed=((d.width, half), BF),
        spread=((d.ncol_b, 16, half), BF),
        mine=((16, half), F32),
        rows_all=((d.nz, 16, half), F32),
        final=((16, half), BF),
        whole=((2, d.width, half), BF),
    )
    semaphores = dict(
        send=24, recv=24, load=4, send_ra=1, send_rb=1, recv_ra=4 * hops_a, recv_rb=4 * hops_b
    )
    semaphores.update(recv_ga=4 * hops_a, recv_gb=4 * hops_b)
    names = tuple(inputs) + tuple(outputs) + tuple(scratch) + tuple(semaphores)
    mixed, feat_grad, weight_raw = pl.pallas_call(
        functools.partial(whole_kernel, d, 1.0 / math.sqrt(node_total), names),
        out_shape=tuple(v[0] for v in outputs.values()),
        in_specs=[v[1] for v in inputs.values()],
        out_specs=tuple(v[1] for v in outputs.values()),
        scratch_shapes=[pltpu.VMEM(*v) for v in scratch.values()]
        + [dma((n,)) for n in semaphores.values()],
        compiler_params=pltpu.CompilerParams(
            collective_id=0, has_side_effects=True, vmem_limit_bytes=LIMIT
        ),
        name="layer",
    )(*(v[0] for v in inputs.values()))
    return pl.pallas_call(
        finish_kernel,
        out_shape=(
            sds(cotangent.shape, BF), sds(feats.shape, BF), sds((d.width, d.width), F32)
        ),
        in_specs=[vmem] * 3,
        out_specs=(vmem,) * 3,
        name="finish",
    )(mixed, feat_grad, weight_raw)


def solution(mesh):
    d = Dims(mesh.shape["row"], mesh.shape["col"])
    placed = (
        P("col", "row"),
        P(),
        P(("row", "col"), None, None),
        P(("row", "col"), None),
        P(("row", "col"), None),
        P(),
        P("col", "row"),
    )
    node_total = d.nrow * d.ncol * 2 * BLK
    return jax.shard_map(
        functools.partial(body, d, node_total),
        mesh=mesh,
        in_specs=placed,
        out_specs=(P("col", "row"), P("col", "row"), P()),
        check_vma=False,
    )
```
